256 devices in a mesh: seg: 64 (over y, z, core), space: 4 (over x).
Axes of the slice: x: 4, y: 4, z: 8, core: 2. Of those that a mesh axis runs over, the one named last changes fastest.
Arguments:
- advect: bfloat16 [64, 4, 4, 256, 512], P('seg', None, 'space'), may hold values from -1 to 1
- growth: bfloat16 [64, 4, 4, 256, 512], P('seg', None, 'space'), may hold values from -0.29882812 to 0.29882812
- forcing: bfloat16 [64, 4, 4, 256, 512], P('seg', None, 'space'), may hold values from -3 to 3
- flux_weight: bfloat16 [64, 4, 4, 256, 512], P('seg', None, 'space'), may hold values from -0.00048828125 to 0.00048828125
- flow_dir: float32 [64, 4, 256, 512], P('seg', 'space'), may hold values from -18 to 18
- helmholtz: float32 [4, 256, 256], P('space'), may hold values from -1 to 2
Outputs:
- multipliers: float32 [64, 4, 256, 512], P('seg', 'space')
- residual: float32 [64, 4, 256, 512], P('seg', 'space')
- sensitivity: float32 [], replicated
The draws below stay inside these ranges and needn't reach their ends.
All inputs are finite; a program needn't handle non-finite values.
Results may differ from the reference program's by a relative error of at most 0.0005.
Values sent between devices are 32-bit elements; how exact they have to be, the bound alone decides.
A program may use at most 64 MiB of HBM per device.

```python
import math
import jax
import jax.numpy as jnp
from jax import lax

NX = 512
NC = 256
STEPS = 4
ITERS = 2
MODES = 4
SEGMENTS = 64


def mode_scales(ratio):
    steps = jnp.arange(MODES).astype(jnp.float32) / max(MODES - 1, 1)
    return (ratio ** steps)[None, :, None, None]


def draw_helmholtz(key, part):
    key = jax.random.fold_in(key, 3)
    noise = jax.random.normal(key, (MODES, NC, NC), jnp.float32)
    return jnp.eye(NC, dtype=jnp.float32)[None] + 0.25 * noise / math.sqrt(NC)


def draw_flow_dir(key, part):
    key = jax.random.fold_in(key, 7)
    shape = (SEGMENTS, MODES, NC, NX)
    values = jnp.clip(jax.random.normal(key, shape, jnp.float32), -6.0, 6.0)
    return values * mode_scales(3.0)


def block_levels(key, dims, pieces, low, largest):
    def one(position, parts):
        draws = jax.random.uniform(jax.random.fold_in(jax.random.fold_in(key, 6), position), (parts,), jnp.float32, low / len(pieces), largest / len(pieces))
        return jnp.repeat(jnp.exp(draws), dims[position] // parts).reshape((-1,) + (1,) * (len(dims) - position - 1))

    factor_of = one(*pieces[0])
    for cut in pieces[1:]:
        factor_of = factor_of * one(*cut)
    return factor_of


def normal_values(rng, dims, deviation, bound, split=(), kind=jnp.bfloat16):
    entries = jax.random.normal(rng, dims, jnp.float32) * deviation
    if len(split) > 0:
        entries = block_levels(rng, dims, split, -0.22, 0.18) * entries
    return jnp.clip(entries, min=-bound, max=bound).astype(kind)


def setup_inputs(seed: int = 0) -> dict:
    key_list = jax.random.split(jax.random.key(seed), 7)
    return {
        "advect": jnp.clip(jax.random.uniform(key_list[0], (SEGMENTS, STEPS, MODES, NC, NX), jnp.float32, -1.0, 1.0) * block_levels(key_list[0], (SEGMENTS, STEPS, MODES, NC, NX), ((0, 64), (2, 4)), -0.4, 0.0), -1.0, 1.0).astype(jnp.bfloat16),
        "growth": jnp.clip(jax.random.uniform(key_list[1], (SEGMENTS, STEPS, MODES, NC, NX), jnp.float32, -0.29882812, 0.29882812) * block_levels(key_list[1], (SEGMENTS, STEPS, MODES, NC, NX), ((0, 64), (2, 4)), -0.4, 0.0), -0.29882812, 0.29882812).astype(jnp.bfloat16),
        "forcing": normal_values(key_list[2], (SEGMENTS, STEPS, MODES, NC, NX), 0.5, 3.0, ((0, 64), (2, 4))),
        "flux_weight": normal_values(key_list[3], (SEGMENTS, STEPS, MODES, NC, NX), (SEGMENTS * STEPS * MODES * NC * NX) ** -0.5, 0.00048828125, ((0, 64), (2, 4))),
        "flow_dir": draw_flow_dir(jax.random.fold_in(key_list[6], 71), 0),
        "helmholtz": draw_helmholtz(jax.random.fold_in(key_list[6], 71), 0),
    }


HIGH = lax.Precision.HIGHEST
EPS = 1e-6


def derive(field):
    width = field.shape[-1]
    waves = jnp.arange(width // 2 + 1)
    waves = jnp.where(waves == width // 2, 0, waves).astype(jnp.float32)
    spectrum = jnp.fft.rfft(field, axis=-1)
    return jnp.fft.irfft(1j * waves * spectrum, n=width, axis=-1).astype(field.dtype)


def tangent_sweep(current, advect, growth, helmholtz, weight, forcing):
    width = current.shape[-1]
    flux = jnp.zeros((current.shape[0],), jnp.float32)
    for time_step in range(advect.shape[1]):
        speed = advect[:, time_step].astype(jnp.float32)
        local_rate = growth[:, time_step].astype(jnp.float32)
        update = current + local_rate * current - speed * derive(current) / width
        if forcing is not None:
            update = update + forcing[:, time_step].astype(jnp.float32)
        current = jnp.einsum("mcd,kmdx->kmcx", helmholtz, update, precision=HIGH)
        flux = flux + jnp.sum(weight[:, time_step].astype(jnp.float32) * current, axis=(1, 2, 3))
    return current, flux


def adjoint_sweep(current, advect, growth, helmholtz):
    width = current.shape[-1]
    for time_step in reversed(range(advect.shape[1])):
        pulled = jnp.einsum("mdc,kmdx->kmcx", helmholtz, current, precision=HIGH)
        speed = advect[:, time_step].astype(jnp.float32)
        local_rate = growth[:, time_step].astype(jnp.float32)
        current = pulled + local_rate * pulled + derive(speed * pulled) / width
    return current


def project(vector, flow, norm):
    factor = jnp.sum(flow * vector, axis=(1, 2, 3)) / norm
    return vector - factor[:, None, None, None] * flow


def reference(advect, growth, forcing, flux_weight, flow_dir, helmholtz):
    segment_count = flow_dir.shape[0]
    active = (jnp.arange(segment_count) < segment_count - 1).astype(jnp.float32)[:, None, None, None]
    norm = jnp.sum(flow_dir * flow_dir, axis=(1, 2, 3)) + EPS
    zeros = jnp.zeros_like(flow_dir)
    source_end, source_flux = tangent_sweep(zeros, advect, growth, helmholtz, flux_weight, forcing)

    def apply(direction):
        pulled = adjoint_sweep(direction, advect, growth, helmholtz)
        before = jnp.concatenate([zeros[:1], direction[:-1]], axis=0)
        kept = project(pulled - before, flow_dir, norm)
        image, flux = tangent_sweep(kept, advect, growth, helmholtz, flux_weight, None)
        after = jnp.concatenate([kept[1:], zeros[:1]], axis=0)
        return (direction + image - after) * active, jnp.sum(flux)

    residual = -source_end * active
    multipliers = zeros
    direction = residual
    size_norm = jnp.sum(residual * residual)
    sensitivity = jnp.sum(source_flux)
    for iteration in range(ITERS):
        applied, term_flux = apply(direction)
        step_size = size_norm / jnp.sum(direction * applied)
        multipliers = multipliers + step_size * direction
        residual = residual - step_size * applied
        sensitivity = sensitivity + step_size * term_flux
        if iteration + 1 < ITERS:
            fresh = jnp.sum(residual * residual)
            direction = residual + (fresh / size_norm) * direction
            size_norm = fresh
    return multipliers, residual, sensitivity
```

```python
import functools
import math

import jax
import jax.numpy as jnp
import numpy as np
from jax import lax
from jax.experimental import pallas as pl
from jax.experimental.pallas import tpu as pltpu
from jax.sharding import PartitionSpec as P

EPS = 1e-06
F32 = jnp.float32
BF16 = jnp.bfloat16
MESH = pl.DeviceIdType.MESH
CHUNKS = 4


def derivative_tables(width):
    offset = np.arange(width)
    angle = np.where(offset == 0, 1, offset) * (math.pi / width)
    wave = 0.5 * np.where(offset % 2 == 0, 1.0, -1.0) / np.tan(angle) / width
    wave[0] = 0.0
    half = width // 2
    index = np.arange(half)
    apart = index[None, :] - index[:, None]
    near, far = wave[apart % width], wave[(apart + half) % width]
    pieces = []
    for table in (0.5 * (near + far), 0.5 * (near - far)):
        high = table.astype(np.float32).astype(jnp.bfloat16)
        pieces += [high, (table - high.astype(np.float64)).astype(np.float32).astype(jnp.bfloat16)]
    return np.stack(pieces)


def dot(a, b):
    return jnp.dot(a, b, preferred_element_type=F32)


def split(x):
    high = x.astype(BF16)
    return high, (x - high.astype(F32)).astype(BF16)


def derive(field, tables):
    half = field.shape[1] // 2
    left, right = field[:, :half], field[:, half:]
    sum_high, sum_low = split(left + right)
    gap_high, gap_low = split(left - right)
    even = dot(sum_high, tables[0]) + dot(sum_low, tables[0]) + dot(sum_high, tables[1])
    odd = dot(gap_high, tables[2]) + dot(gap_low, tables[2]) + dot(gap_high, tables[3])
    return jnp.concatenate([even + odd, even - odd], axis=1)


def mix(matrix, field):
    high, low = split(field)
    return dot(matrix[0], high) + dot(matrix[1], high) + dot(matrix[0], low)


def lanes(product):
    row = jnp.sum(product, axis=0, keepdims=True)
    return sum(row[:, k : k + 128] for k in range(0, row.shape[1], 128))


def total(row):
    return jnp.sum(row, axis=1, keepdims=True)


def kernel(
    groups, advect_in, growth_in, forcing_in, weight_in, flow_in, helm_in, tables_in,
    mult_out, res_out, sens_out,
    advect, growth, forcing, weight, flow, helm, tables, matrix,
    state, p0, w0, y0, s1, w1, tang_flow, grad, v1,
    flow_next, p_prev, w0_next, y_prev, w1_next,
    near_own, near_next, plane, line, line_next,
    load_sem, send_sem, recv_sem,
    near_send, near_recv, next_recv, plane_send, plane_recv, line_send, line_recv, line_next_sem,
):
    seg_count, space_count, rows = groups
    seg, space = lax.axis_index("seg"), lax.axis_index("space")
    after, before = lax.rem(seg + 1, seg_count), lax.rem(seg + seg_count - 1, seg_count)
    steps, height, width = advect.shape
    planes = seg_count // rows
    active = jnp.where(seg < seg_count - 1, 1.0, 0.0).astype(F32)
    not_first = jnp.where(seg > 0, 1.0, 0.0).astype(F32)

    def load(slot, source, target):
        return pltpu.make_async_copy(source, target, load_sem.at[slot])

    def step_loads(n):
        return (
            load(n, forcing_in.at[n], forcing.at[n]),
            load(steps + n, advect_in.at[n], advect.at[n]),
            load(2 * steps + n, growth_in.at[n], growth.at[n]),
        )

    base = 3 * steps
    load_helm = load(base, helm_in, helm)
    load_tables = load(base + 1, tables_in, tables)
    load_flow = load(base + 2, flow_in, flow)
    load_weight = load(base + 3, weight_in, weight)
    load_helm.start()
    step_loads(0)[0].start()
    load_tables.start()
    for n in range(1, steps):
        for copy in step_loads(n):
            copy.start()
    for copy in step_loads(0)[1:]:
        copy.start()
    load_flow.start()
    load_weight.start()

    plane_me = (seg // rows) * space_count + space
    line_me = lax.rem(seg, rows)
    plane_size, line_size = planes * space_count, rows

    def plane_peer(d):
        j = lax.rem(plane_me + d, plane_size)
        return j, (lax.div(j, space_count) * rows + line_me, lax.rem(j, space_count))

    def line_peer(d):
        j = lax.rem(line_me + d, line_size)
        return j, ((seg // rows) * rows + j, space)

    barrier = pltpu.get_barrier_semaphore()
    greeted = [plane_peer(d)[1] for d in range(1, plane_size)]
    greeted += [line_peer(d)[1] for d in range(1, line_size)]
    greeted += [(s, lax.rem(space + d, space_count)) for s in (before, after) for d in range(space_count)]
    for peer in greeted:
        pl.semaphore_signal(barrier, inc=1, device_id=peer, device_id_type=MESH)

    piece = height // CHUNKS

    def transfer(kind, source, target, seg_to):
        return [
            pltpu.make_async_remote_copy(
                src_ref=source.at[pl.ds(c * piece, piece), :],
                dst_ref=target.at[pl.ds(c * piece, piece), :],
                send_sem=send_sem.at[kind, c],
                recv_sem=recv_sem.at[kind, c],
                device_id=(seg_to, space),
                device_id_type=MESH,
            )
            for c in range(CHUNKS)
        ]

    def start(copies):
        for copy in copies:
            copy.start()

    def arrived(copies):
        for copy in copies:
            copy.wait_recv()

    send_flow = transfer(0, flow_in, flow_next, before)
    send_p0 = transfer(1, p0, p_prev, after)
    send_w0 = transfer(2, w0, w0_next, before)
    send_y0 = transfer(3, y0, y_prev, after)
    send_w1 = transfer(4, w1, w1_next, before)

    def spread(d_table):
        return [tables[k] for k in range(4)]

    def forward():
        return matrix[0], matrix[1]

    def backward():
        return matrix[2], matrix[3]

    def tangent_step(n, forced):
        now = state[...]
        rate = growth[n].astype(F32)
        speed = advect[n].astype(F32)
        update = now + rate * now - speed * derive(now, spread(0))
        if forced:
            update = update + forcing[n].astype(F32)
        state[...] = mix(forward(), update)

    def adjoint_rest(n, pulled):
        rate = growth[n].astype(F32)
        speed = advect[n].astype(F32)
        return pulled + rate * pulled + derive(speed * pulled, spread(0))

    def tangent_sweep(first, last):
        @pl.loop(first, last)
        def _(n):
            tangent_step(n, False)

    def adjoint_sweep():
        @pl.loop(0, steps)
        def _(k):
            state[...] = adjoint_rest(steps - 1 - k, mix(backward(), state[...]))

    load_helm.wait()
    high, low = split(helm[...])
    matrix[0], matrix[1] = high, low
    high, low = split(helm[...].T)
    matrix[2], matrix[3] = high, low
    step_loads(0)[0].wait()
    state[...] = dot(matrix[0], forcing[0]) + dot(matrix[1], forcing[0])
    pl.semaphore_wait(barrier, len(greeted))
    start(send_flow)
    load_tables.wait()

    @pl.loop(1, steps)
    def _(n):
        for copy in step_loads(n):
            copy.wait()
        tangent_step(n, True)

    p0[...] = -active * state[...]
    start(send_p0)

    for copy in step_loads(0)[1:]:
        copy.wait()
    state[...] = p0[...]
    adjoint_sweep()
    w0[...] = state[...]
    start(send_w0)

    load_flow.wait()
    state[...] = flow[...]
    tangent_sweep(0, steps)
    tang_flow[...] = state[...]

    load_weight.wait()
    state[...] = jnp.zeros_like(state)

    def gradient_step(k, flux):
        n = steps - 1 - k
        pulled = mix(backward(), weight[n].astype(F32) + state[...])
        state[...] = adjoint_rest(n, pulled)
        return flux + lanes(pulled * forcing[n].astype(F32))

    flux_row = lax.fori_loop(0, steps, gradient_step, jnp.zeros((1, 128), F32))
    grad[...] = state[...]

    ff_row = lanes(flow[...] * flow[...])
    gf_row = lanes(grad[...] * flow[...])
    pp_row = lanes(p0[...] * p0[...])

    arrived(send_p0)
    state[...] = w0[...] - p_prev[...]
    fv0_row = lanes(flow[...] * state[...])
    near_own[space] = jnp.concatenate([ff_row, fv0_row, jnp.zeros((6, 128), F32)], axis=0)
    near_copies = []
    for d in range(1, space_count):
        j = lax.rem(space + d, space_count)
        near_copies.append(
            (
                pltpu.make_async_remote_copy(
                    src_ref=near_own.at[space], dst_ref=near_own.at[space], send_sem=near_send.at[d - 1],
                    recv_sem=near_recv.at[space], device_id=(seg, j), device_id_type=MESH,
                ),
                pltpu.make_async_remote_copy(
                    src_ref=near_own.at[j], dst_ref=near_own.at[j], send_sem=near_send.at[d - 1],
                    recv_sem=near_recv.at[j], device_id=(seg, j), device_id_type=MESH,
                ),
            )
        )
    for d in range(space_count):
        j = lax.rem(space + d, space_count)
        near_copies.append(
            (
                pltpu.make_async_remote_copy(
                    src_ref=near_own.at[space], dst_ref=near_next.at[space],
                    send_sem=near_send.at[space_count - 1 + d], recv_sem=next_recv.at[space],
                    device_id=(before, j), device_id_type=MESH,
                ),
                pltpu.make_async_remote_copy(
                    src_ref=near_own.at[j], dst_ref=near_next.at[j],
                    send_sem=near_send.at[space_count - 1 + d], recv_sem=next_recv.at[j],
                    device_id=(before, j), device_id_type=MESH,
                ),
            )
        )
    for copy, _ in near_copies:
        copy.start()
    vv0_row = lanes(state[...] * state[...])
    gv0_row = lanes(grad[...] * state[...])
    tangent_sweep(0, steps)
    for _, copy in near_copies:
        copy.wait_recv()
    sums = near_own[0] + near_own[1] + near_own[2] + near_own[3]
    c0 = total(sums[1:2]) / (total(sums[0:1]) + EPS)
    sums = near_next[0] + near_next[1] + near_next[2] + near_next[3]
    c0_next = total(sums[1:2]) / (total(sums[0:1]) + EPS)
    y0[...] = state[...] - c0 * tang_flow[...]
    start(send_y0)

    arrived(send_w0)
    arrived(send_flow)
    s1[...] = active * (2.0 * p0[...] + y0[...] - w0_next[...] + c0_next * flow_next[...])
    state[...] = s1[...]
    adjoint_sweep()
    w1[...] = state[...]
    start(send_w1)
    ss_row = lanes(s1[...] * s1[...])

    arrived(send_y0)
    state[...] = w1[...] - not_first * (2.0 * p_prev[...] + y_prev[...] - w0[...] + c0 * flow[...])
    v1_rows = [lanes(other * state[...]) for other in (flow[...], state[...], grad[...])]
    plane[plane_me] = jnp.concatenate(
        [ff_row, gf_row, fv0_row, vv0_row, gv0_row, *v1_rows, pp_row, ss_row, flux_row, jnp.zeros((5, 128), F32)],
        axis=0,
    )

    def plane_copy(d):
        j, peer = plane_peer(d)
        send = pltpu.make_async_remote_copy(
            src_ref=plane.at[plane_me], dst_ref=plane.at[plane_me], send_sem=plane_send.at[d],
            recv_sem=plane_recv.at[plane_me], device_id=peer, device_id_type=MESH,
        )
        receive = pltpu.make_async_remote_copy(
            src_ref=plane.at[j], dst_ref=plane.at[j], send_sem=plane_send.at[d],
            recv_sem=plane_recv.at[j], device_id=peer, device_id_type=MESH,
        )
        return send, receive

    plane_copies = [plane_copy(d) for d in range(1, plane_size)]
    for copy, _ in plane_copies:
        copy.start()
    tangent_sweep(0, steps - 1)
    for _, copy in plane_copies:
        copy.wait_recv()

    def group_sums(k):
        tile = plane[k * space_count]
        for x in range(1, space_count):
            tile = tile + plane[k * space_count + x]
        return jnp.sum(tile, axis=1, keepdims=True)

    def group_terms(k):
        s = group_sums(k)
        norm, gf, fv0, vv0, gv0, fv1, vv1, gv1, pp, ss, flux = [s[r : r + 1] for r in range(11)]
        norm = norm + EPS
        a, b = fv0 / norm, fv1 / norm
        return [pp, vv0 - a * fv0, gv0 - a * gf, ss, vv1 - b * fv1, gv1 - b * gf, flux, b]

    terms = [group_terms(k) for k in range(planes)]
    summed = [sum(t[r] for t in terms[1:]) + terms[0][r] for r in range(7)]
    c1 = group_terms(seg // rows)[7]
    line[line_me] = jnp.concatenate([jnp.broadcast_to(t, (1, 128)) for t in [*summed, c1]], axis=0)

    def line_copy(d):
        j, peer = line_peer(d)
        send = pltpu.make_async_remote_copy(
            src_ref=line.at[line_me], dst_ref=line.at[line_me], send_sem=line_send.at[d],
            recv_sem=line_recv.at[line_me], device_id=peer, device_id_type=MESH,
        )
        receive = pltpu.make_async_remote_copy(
            src_ref=line.at[j], dst_ref=line.at[j], send_sem=line_send.at[d],
            recv_sem=line_recv.at[j], device_id=peer, device_id_type=MESH,
        )
        return send, receive

    line_copies = [line_copy(d) for d in range(1, line_size)]
    to_before = pltpu.make_async_remote_copy(
        src_ref=line.at[line_me], dst_ref=line_next, send_sem=line_send.at[0],
        recv_sem=line_next_sem, device_id=(before, space), device_id_type=MESH,
    )
    to_before.start()
    for copy, _ in line_copies:
        copy.start()
    tangent_sweep(steps - 1, steps)
    for _, copy in line_copies:
        copy.wait_recv()
    to_before.wait_recv()

    whole = line[0]
    for k in range(1, line_size):
        whole = whole + line[k]
    rr, q0, g0, m11, q1, g1, flux = [whole[r : r + 1, 0:1] for r in range(7)]
    c1_next = line_next[7:8, 0:1]
    k0 = rr + q0
    k11 = m11 + q1
    alpha0 = rr / k0
    fresh = alpha0 * alpha0 * m11 - rr
    beta = fresh / rr
    more = 1.0 + beta
    alpha1 = fresh / (more * more * k0 - 2.0 * alpha0 * more * m11 + alpha0 * alpha0 * k11)
    sens = flux + alpha0 * g0 + alpha1 * (more * g0 - alpha0 * g1)
    sens_out[...] = jnp.broadcast_to(sens, sens_out.shape)

    mult_out[...] = (alpha0 + alpha1 * more) * p0[...] - (alpha1 * alpha0) * s1[...]
    arrived(send_w1)
    s2 = 2.0 * s1[...] + state[...] - c1 * tang_flow[...] - w1_next[...] + c1_next * flow_next[...]
    res_out[...] = active * (
        p0[...] - (alpha0 + alpha1 * more) * s1[...] + (alpha1 * alpha0) * s2
    )

    for copies in (send_flow, send_p0, send_w0, send_y0, send_w1):
        for copy in copies:
            copy.wait_send()
    for copy, _ in near_copies + plane_copies + line_copies:
        copy.wait_send()
    to_before.wait_send()


def on_device(rows, axes, advect, growth, forcing, flux_weight, flow_dir, helmholtz):
    steps, height, width = advect.shape[1], advect.shape[3], advect.shape[4]
    seg_count, space_count = axes
    planes = seg_count // rows
    plane_size = planes * space_count
    field = pltpu.VMEM((height, width), F32)
    steps_bf16 = pltpu.VMEM((steps, height, width), BF16)
    half = width // 2
    dma = pltpu.SemaphoreType.DMA
    shape = (steps, height, width)
    mult, res, sens = pl.pallas_call(
        functools.partial(kernel, (seg_count, space_count, rows)),
        out_shape=(
            jax.ShapeDtypeStruct((height, width), F32),
            jax.ShapeDtypeStruct((height, width), F32),
            jax.ShapeDtypeStruct((8, 128), F32),
        ),
        in_specs=[pl.BlockSpec(memory_space=pl.ANY)] * 7,
        out_specs=tuple([pl.BlockSpec(memory_space=pltpu.VMEM)] * 3),
        scratch_shapes=[
            steps_bf16, steps_bf16, steps_bf16, steps_bf16, field,
            pltpu.VMEM((height, height), F32), pltpu.VMEM((4, half, half), BF16),
            pltpu.VMEM((4, height, height), BF16),
            *[field] * 9,
            *[field] * 5,
            pltpu.VMEM((space_count, 8, 128), F32), pltpu.VMEM((space_count, 8, 128), F32),
            pltpu.VMEM((plane_size, 16, 128), F32), pltpu.VMEM((rows, 8, 128), F32), pltpu.VMEM((8, 128), F32),
            dma((3 * steps + 4,)), dma((5, CHUNKS)), dma((5, CHUNKS)),
            dma((2 * space_count - 1,)), dma((space_count,)), dma((space_count,)),
            dma((plane_size,)), dma((plane_size,)), dma((rows,)), dma((rows,)), dma,
        ],
        compiler_params=pltpu.CompilerParams(
            collective_id=0, has_side_effects=True, vmem_limit_bytes=48 << 20
        ),
        cost_estimate=pl.CostEstimate(flops=8_000_000_000, bytes_accessed=6_000_000, transcendentals=0),
    )(
        advect.reshape(shape), growth.reshape(shape), forcing.reshape(shape), flux_weight.reshape(shape),
        flow_dir.reshape(height, width), helmholtz.reshape(height, height),
        jnp.asarray(derivative_tables(width)),
    )
    return mult[None, None], res[None, None], sens[0, 0]


def solution(mesh):
    in_specs = (
        P("seg", None, "space", None, None),
        P("seg", None, "space", None, None),
        P("seg", None, "space", None, None),
        P("seg", None, "space", None, None),
        P("seg", "space", None, None),
        P("space", None, None),
    )
    out_specs = (P("seg", "space", None, None), P("seg", "space", None, None), P())
    axes = (mesh.shape["seg"], mesh.shape["space"])
    rows = 16 if axes[0] % 16 == 0 else axes[0]
    return jax.shard_map(
        functools.partial(on_device, rows, axes), mesh=mesh, in_specs=in_specs, out_specs=out_specs, check_vma=False
    )
```

```python
import functools
import math

import jax
import jax.numpy as jnp
from jax import lax
from jax.experimental import pallas as pl
from jax.experimental.pallas import tpu as pltpu
from jax.sharding import PartitionSpec as P

EPS = 1e-06
F32 = jnp.float32
BF16 = jnp.bfloat16
MESH = pl.DeviceIdType.MESH
CHUNKS = 4


def cotangent(angle):
    square = angle * angle
    sine = jnp.ones_like(angle)
    for n in (13, 11, 9, 7, 5, 3):
        sine = 1.0 - square * sine * (1.0 / (n * (n - 1)))
    cosine = jnp.ones_like(angle)
    for n in (14, 12, 10, 8, 6, 4, 2):
        cosine = 1.0 - square * cosine * (1.0 / (n * (n - 1)))
    return cosine / (angle * sine)


def derivative_tables(width):
    half = width // 2
    column = lax.broadcasted_iota(jnp.int32, (8, width), 1)
    apart = jnp.where(column < half, column, width - column)
    inside = jnp.logical_and(apart > 0, apart < half)
    apart = jnp.where(inside, apart, 1)
    step = math.pi / width
    near = cotangent(apart.astype(F32) * step)
    far = cotangent((half - apart).astype(F32) * step)
    sign = jnp.where((column < half) == (apart % 2 == 0), 0.25 / width, -0.25 / width)
    sign = jnp.where(inside, sign, 0.0)
    tables = []
    for row in (sign * (near - far), sign * (near + far)):
        block = jnp.concatenate([row] * (half // 8), axis=0)
        tables.append(pltpu.roll(block, 0, 1, stride=1, stride_axis=0)[:, :half])
    return tables


def dot(a, b):
    return jnp.dot(a, b, preferred_element_type=F32)


def split(x):
    high = x.astype(BF16)
    return high, (x - high.astype(F32)).astype(BF16)


def derive(field, tables):
    half = field.shape[1] // 2
    left, right = field[:, :half], field[:, half:]
    sum_high, sum_low = split(left + right)
    gap_high, gap_low = split(left - right)
    even = dot(sum_high, tables[0]) + dot(sum_low, tables[0]) + dot(sum_high, tables[1])
    odd = dot(gap_high, tables[2]) + dot(gap_low, tables[2]) + dot(gap_high, tables[3])
    return jnp.concatenate([even + odd, even - odd], axis=1)


def mix(matrix, field):
    high, low = split(field)
    return dot(matrix[0], high) + dot(matrix[1], high) + dot(matrix[0], low)


def lanes(product):
    row = jnp.sum(product, axis=0, keepdims=True)
    return sum(row[:, k : k + 128] for k in range(0, row.shape[1], 128))


def total(row):
    return jnp.sum(row, axis=1, keepdims=True)


def kernel(
    groups, advect_in, growth_in, forcing_in, weight_in, flow_in, helm_in,
    mult_out, res_out, sens_out,
    advect, growth, forcing, weight, flow, helm, tables, matrix,
    state, other, p0, w0, y0, s1, w1, tang_flow, grad,
    flow_next, p_prev, w0_next, y_prev, w1_next,
    near_own, near_next, plane, line, line_next, coef,
    load_sem, send_sem, recv_sem,
    near_send, near_recv, next_recv, plane_send, plane_recv, line_send, line_recv, line_next_sem,
):
    seg_count, space_count, rows = groups
    seg, space = lax.axis_index("seg"), lax.axis_index("space")
    after, before = lax.rem(seg + 1, seg_count), lax.rem(seg + seg_count - 1, seg_count)
    steps, height, width = advect.shape
    planes = seg_count // rows
    active = jnp.where(seg < seg_count - 1, 1.0, 0.0).astype(F32)
    not_first = jnp.where(seg > 0, 1.0, 0.0).astype(F32)

    def load(slot, source, target):
        return pltpu.make_async_copy(source, target, load_sem.at[slot])

    def load_forcing(n):
        return load(n, forcing_in.at[n], forcing.at[n])

    def step_loads(n):
        return (
            load(steps + n, advect_in.at[n], advect.at[n]),
            load(2 * steps + n, growth_in.at[n], growth.at[n]),
        )

    base = 3 * steps
    load_helm = load(base, helm_in, helm)
    load_flow = load(base + 1, flow_in, flow)
    load_weight = load(base + 2, weight_in, weight)
    load_helm.start()
    load_forcing(0).start()
    for n in range(1, steps):
        for copy in (load_forcing(n), *step_loads(n)):
            copy.start()
    for copy in step_loads(0):
        copy.start()
    load_flow.start()
    load_weight.start()

    plane_me = (seg // rows) * space_count + space
    line_me = lax.rem(seg, rows)
    plane_size, line_size = planes * space_count, rows

    def plane_peer(d):
        j = lax.rem(plane_me + d, plane_size)
        return j, (lax.div(j, space_count) * rows + line_me, lax.rem(j, space_count))

    def line_peer(d):
        j = lax.rem(line_me + d, line_size)
        return j, ((seg // rows) * rows + j, space)

    barrier = pltpu.get_barrier_semaphore()
    greeted = [plane_peer(d)[1] for d in range(1, plane_size)]
    greeted += [line_peer(d)[1] for d in range(1, line_size)]
    greeted += [(s, lax.rem(space + d, space_count)) for s in (before, after) for d in range(space_count)]
    for peer in greeted:
        pl.semaphore_signal(barrier, inc=1, device_id=peer, device_id_type=MESH)

    piece = height // CHUNKS

    def transfer(kind, source, target, seg_to):
        return [
            pltpu.make_async_remote_copy(
                src_ref=source.at[pl.ds(c * piece, piece), :],
                dst_ref=target.at[pl.ds(c * piece, piece), :],
                send_sem=send_sem.at[kind, c],
                recv_sem=recv_sem.at[kind, c],
                device_id=(seg_to, space),
                device_id_type=MESH,
            )
            for c in range(CHUNKS)
        ]

    def start(copies):
        for copy in copies:
            copy.start()

    def arrived(copies):
        for copy in copies:
            copy.wait_recv()

    send_flow = transfer(0, flow_in, flow_next, before)
    send_p0 = transfer(1, p0, p_prev, after)
    send_w0 = transfer(2, w0, w0_next, before)
    send_y0 = transfer(3, y0, y_prev, after)
    send_w1 = transfer(4, w1, w1_next, before)

    def forward():
        return matrix[0], matrix[1]

    def backward():
        return matrix[2], matrix[3]

    def tangent(n, now, forced=False):
        rate = growth[n].astype(F32)
        speed = advect[n].astype(F32)
        update = now + rate * now - speed * derive(now, [tables[k] for k in range(4)])
        if forced:
            update = update + forcing[n].astype(F32)
        return mix(forward(), update)

    def adjoint_rest(n, pulled):
        rate = growth[n].astype(F32)
        speed = advect[n].astype(F32)
        return pulled + rate * pulled + derive(speed * pulled, [tables[k] for k in range(4)])

    def tangent_sweep(first, last):
        @pl.loop(first, last)
        def _(n):
            state[...] = tangent(n, state[...])

    def adjoint_sweep():
        @pl.loop(0, steps)
        def _(k):
            state[...] = adjoint_rest(steps - 1 - k, mix(backward(), state[...]))

    def gradient_step(k, now, flux):
        n = steps - 1 - k
        pulled = mix(backward(), weight[n].astype(F32) + now)
        return adjoint_rest(n, pulled), flux + lanes(pulled * forcing[n].astype(F32))

    def put(row, value):
        plane[plane_me, pl.ds(row, 1), :] = value

    for k, table in enumerate(derivative_tables(width)):
        tables[2 * k], tables[2 * k + 1] = split(table)

    load_helm.wait()
    high, low = split(helm[...])
    matrix[0], matrix[1] = high, low
    load_forcing(0).wait()
    state[...] = dot(matrix[0], forcing[0]) + dot(matrix[1], forcing[0])
    high, low = split(helm[...].T)
    matrix[2], matrix[3] = high, low
    pl.semaphore_wait(barrier, len(greeted))
    start(send_flow)

    @pl.loop(1, steps)
    def _(n):
        for copy in (load_forcing(n), *step_loads(n)):
            copy.wait()
        state[...] = tangent(n, state[...], forced=True)

    for c in range(CHUNKS):
        part = pl.ds(c * piece, piece)
        p0[part, :] = -active * state[part, :]
        send_p0[c].start()

    for copy in step_loads(0):
        copy.wait()
    state[...] = p0[...]
    adjoint_sweep()
    w0[...] = state[...]
    start(send_w0)
    load_flow.wait()
    load_weight.wait()
    put(0, lanes(flow[...] * flow[...]))
    put(8, lanes(p0[...] * p0[...]))
    plane[plane_me, pl.ds(11, 5), :] = jnp.zeros((5, 128), F32)

    def near_pairs():
        pairs = []
        for d in range(2 * space_count):
            own = d < space_count
            if d == 0:
                continue
            j = lax.rem(space + d, space_count)
            kept, sems = (near_own, near_recv) if own else (near_next, next_recv)
            to = (seg if own else before, j)
            pairs.append(
                (
                    pltpu.make_async_remote_copy(
                        src_ref=near_own.at[space], dst_ref=kept.at[space], send_sem=near_send.at[d - 1],
                        recv_sem=sems.at[space], device_id=to, device_id_type=MESH,
                    ),
                    pltpu.make_async_remote_copy(
                        src_ref=near_own.at[space], dst_ref=kept.at[j], send_sem=near_send.at[d - 1],
                        recv_sem=sems.at[j], device_id=to, device_id_type=MESH,
                    ),
                )
            )
        return pairs

    near_copies = near_pairs()

    def begin_v0():
        arrived(send_p0)
        state[...] = w0[...] - p_prev[...]
        row = lanes(flow[...] * state[...])
        put(2, row)
        near_own[space] = jnp.concatenate(
            [plane[plane_me, pl.ds(0, 1), :], row, jnp.zeros((6, 128), F32)], axis=0
        )
        for copy, _ in near_copies:
            copy.start()
        put(3, lanes(state[...] * state[...]))

    def end_y0():
        for _, copy in near_copies:
            copy.wait_recv()
        for row, kept in ((0, near_own), (1, near_next)):
            sums = kept[0]
            for x in range(1, space_count):
                sums = sums + kept[x]
            c = total(sums[1:2]) / (total(sums[0:1]) + EPS)
            coef[pl.ds(row, 1), :] = jnp.broadcast_to(c, (1, 128))
        c0 = coef[0:1, 0:1]
        for c in range(CHUNKS):
            part = pl.ds(c * piece, piece)
            y0[part, :] = state[part, :] - c0 * tang_flow[part, :]
            send_y0[c].start()

    second = lax.rem(seg, 2) == 1

    @pl.when(second)
    def _():
        begin_v0()
        other[...] = flow[...]

        @pl.loop(0, steps)
        def _(n):
            one, two = tangent(n, state[...]), tangent(n, other[...])
            state[...] = one
            other[...] = two

        tang_flow[...] = other[...]
        end_y0()
        other[...] = jnp.zeros_like(other)

        def body(k, flux):
            now, flux = gradient_step(k, other[...], flux)
            other[...] = now
            return flux

        put(10, lax.fori_loop(0, steps, body, jnp.zeros((1, 128), F32)))
        grad[...] = other[...]

    @pl.when(jnp.logical_not(second))
    def _():
        other[...] = flow[...]
        state[...] = jnp.zeros_like(state)

        def body(k, flux):
            one = tangent(k, other[...])
            now, flux = gradient_step(k, state[...], flux)
            other[...] = one
            state[...] = now
            return flux

        put(10, lax.fori_loop(0, steps, body, jnp.zeros((1, 128), F32)))
        tang_flow[...] = other[...]
        grad[...] = state[...]
        begin_v0()
        tangent_sweep(0, steps)
        end_y0()

    put(1, lanes(grad[...] * flow[...]))
    put(4, lanes(grad[...] * (w0[...] - p_prev[...])))
    c0, c0_next = coef[0:1, 0:1], coef[1:2, 0:1]

    arrived(send_w0)
    arrived(send_flow)
    s1[...] = active * (2.0 * p0[...] + y0[...] - w0_next[...] + c0_next * flow_next[...])
    state[...] = s1[...]
    adjoint_sweep()
    w1[...] = state[...]
    start(send_w1)
    put(9, lanes(s1[...] * s1[...]))

    arrived(send_y0)
    state[...] = w1[...] - not_first * (2.0 * p_prev[...] + y_prev[...] - w0[...] + c0 * flow[...])
    for row, factor in ((5, flow), (6, state), (7, grad)):
        put(row, lanes(factor[...] * state[...]))

    def plane_copy(d):
        j, peer = plane_peer(d)
        send = pltpu.make_async_remote_copy(
            src_ref=plane.at[plane_me], dst_ref=plane.at[plane_me], send_sem=plane_send.at[d],
            recv_sem=plane_recv.at[plane_me], device_id=peer, device_id_type=MESH,
        )
        receive = pltpu.make_async_remote_copy(
            src_ref=plane.at[j], dst_ref=plane.at[j], send_sem=plane_send.at[d],
            recv_sem=plane_recv.at[j], device_id=peer, device_id_type=MESH,
        )
        return send, receive

    plane_copies = [plane_copy(d) for d in range(1, plane_size)]
    for copy, _ in plane_copies:
        copy.start()
    tangent_sweep(0, steps - 1)
    for _, copy in plane_copies:
        copy.wait_recv()

    def group_sums(k):
        tile = plane[k * space_count]
        for x in range(1, space_count):
            tile = tile + plane[k * space_count + x]
        return jnp.sum(tile, axis=1, keepdims=True)

    def group_terms(k):
        s = group_sums(k)
        norm, gf, fv0, vv0, gv0, fv1, vv1, gv1, pp, ss, flux = [s[r : r + 1] for r in range(11)]
        norm = norm + EPS
        a, b = fv0 / norm, fv1 / norm
        return [pp, vv0 - a * fv0, gv0 - a * gf, ss, vv1 - b * fv1, gv1 - b * gf, flux, b]

    terms = [group_terms(k) for k in range(planes)]
    summed = [sum(t[r] for t in terms[1:]) + terms[0][r] for r in range(7)]
    c1 = group_terms(seg // rows)[7]
    line[line_me] = jnp.concatenate([jnp.broadcast_to(t, (1, 128)) for t in [*summed, c1]], axis=0)

    def line_copy(d):
        j, peer = line_peer(d)
        send = pltpu.make_async_remote_copy(
            src_ref=line.at[line_me], dst_ref=line.at[line_me], send_sem=line_send.at[d],
            recv_sem=line_recv.at[line_me], device_id=peer, device_id_type=MESH,
        )
        receive = pltpu.make_async_remote_copy(
            src_ref=line.at[j], dst_ref=line.at[j], send_sem=line_send.at[d],
            recv_sem=line_recv.at[j], device_id=peer, device_id_type=MESH,
        )
        return send, receive

    line_copies = [line_copy(d) for d in range(1, line_size)]
    to_before = pltpu.make_async_remote_copy(
        src_ref=line.at[line_me], dst_ref=line_next, send_sem=line_send.at[0],
        recv_sem=line_next_sem, device_id=(before, space), device_id_type=MESH,
    )
    to_before.start()
    for copy, _ in line_copies:
        copy.start()
    tangent_sweep(steps - 1, steps)
    for _, copy in line_copies:
        copy.wait_recv()
    to_before.wait_recv()

    whole = line[0]
    for k in range(1, line_size):
        whole = whole + line[k]
    rr, q0, g0, m11, q1, g1, flux = [whole[r : r + 1, 0:1] for r in range(7)]
    c1_next = line_next[7:8, 0:1]
    k0 = rr + q0
    k11 = m11 + q1
    alpha0 = rr / k0
    fresh = alpha0 * alpha0 * m11 - rr
    beta = fresh / rr
    more = 1.0 + beta
    alpha1 = fresh / (more * more * k0 - 2.0 * alpha0 * more * m11 + alpha0 * alpha0 * k11)
    sens = flux + alpha0 * g0 + alpha1 * (more * g0 - alpha0 * g1)
    sens_out[...] = jnp.broadcast_to(sens, sens_out.shape)

    mult_out[...] = (alpha0 + alpha1 * more) * p0[...] - (alpha1 * alpha0) * s1[...]
    arrived(send_w1)
    s2 = 2.0 * s1[...] + state[...] - c1 * tang_flow[...] - w1_next[...] + c1_next * flow_next[...]
    res_out[...] = active * (
        p0[...] - (alpha0 + alpha1 * more) * s1[...] + (alpha1 * alpha0) * s2
    )

    for copies in (send_flow, send_p0, send_w0, send_y0, send_w1):
        for copy in copies:
            copy.wait_send()
    for copy, _ in near_copies + plane_copies + line_copies:
        copy.wait_send()
    to_before.wait_send()


def on_device(rows, axes, advect, growth, forcing, flux_weight, flow_dir, helmholtz):
    steps, height, width = advect.shape[1], advect.shape[3], advect.shape[4]
    seg_count, space_count = axes
    planes = seg_count // rows
    plane_size = planes * space_count
    field = pltpu.VMEM((height, width), F32)
    steps_bf16 = pltpu.VMEM((steps, height, width), BF16)
    half = width // 2
    dma = pltpu.SemaphoreType.DMA
    shape = (steps, height, width)
    mult, res, sens = pl.pallas_call(
        functools.partial(kernel, (seg_count, space_count, rows)),
        out_shape=(
            jax.ShapeDtypeStruct((height, width), F32),
            jax.ShapeDtypeStruct((height, width), F32),
            jax.ShapeDtypeStruct((8, 128), F32),
        ),
        in_specs=[pl.BlockSpec(memory_space=pl.ANY)] * 6,
        out_specs=tuple([pl.BlockSpec(memory_space=pltpu.VMEM)] * 3),
        scratch_shapes=[
            steps_bf16, steps_bf16, steps_bf16, steps_bf16, field,
            pltpu.VMEM((height, height), F32), pltpu.VMEM((4, half, half), BF16),
            pltpu.VMEM((4, height, height), BF16),
            *[field] * 9,
            *[field] * 5,
            pltpu.VMEM((space_count, 8, 128), F32), pltpu.VMEM((space_count, 8, 128), F32),
            pltpu.VMEM((plane_size, 16, 128), F32), pltpu.VMEM((rows, 8, 128), F32), pltpu.VMEM((8, 128), F32), pltpu.VMEM((8, 128), F32),
            dma((3 * steps + 3,)), dma((5, CHUNKS)), dma((5, CHUNKS)),
            dma((2 * space_count - 1,)), dma((space_count,)), dma((space_count,)),
            dma((plane_size,)), dma((plane_size,)), dma((rows,)), dma((rows,)), dma,
        ],
        compiler_params=pltpu.CompilerParams(
            collective_id=0, has_side_effects=True, vmem_limit_bytes=60 << 20
        ),
        cost_estimate=pl.CostEstimate(flops=8_000_000_000, bytes_accessed=6_000_000, transcendentals=0),
    )(
        advect.reshape(shape), growth.reshape(shape), forcing.reshape(shape), flux_weight.reshape(shape),
        flow_dir.reshape(height, width), helmholtz.reshape(height, height),
    )
    return mult[None, None], res[None, None], sens[0, 0]


def solution(mesh):
    in_specs = (
        P("seg", None, "space", None, None),
        P("seg", None, "space", None, None),
        P("seg", None, "space", None, None),
        P("seg", None, "space", None, None),
        P("seg", "space", None, None),
        P("space", None, None),
    )
    out_specs = (P("seg", "space", None, None), P("seg", "space", None, None), P())
    axes = (mesh.shape["seg"], mesh.shape["space"])
    rows = 16 if axes[0] % 16 == 0 else axes[0]
    return jax.shard_map(
        functools.partial(on_device, rows, axes), mesh=mesh, in_specs=in_specs, out_specs=out_specs, check_vma=False
    )
```

```python
import functools
import math

import jax
import jax.numpy as jnp
from jax import lax
from jax.experimental import pallas as pl
from jax.experimental.pallas import tpu as pltpu
from jax.sharding import PartitionSpec as P

EPS = 1e-06
F32 = jnp.float32
BF16 = jnp.bfloat16
MESH = pl.DeviceIdType.MESH
CHUNKS = 4


def cotangent(angle):
    square = angle * angle
    sine = jnp.ones_like(angle)
    for n in (13, 11, 9, 7, 5, 3):
        sine = 1.0 - square * sine * (1.0 / (n * (n - 1)))
    cosine = jnp.ones_like(angle)
    for n in (14, 12, 10, 8, 6, 4, 2):
        cosine = 1.0 - square * cosine * (1.0 / (n * (n - 1)))
    return cosine / (angle * sine)


def derivative_tables(width):
    half = width // 2
    column = lax.broadcasted_iota(jnp.int32, (8, width), 1)
    apart = jnp.where(column < half, column, width - column)
    inside = jnp.logical_and(apart > 0, apart < half)
    apart = jnp.where(inside, apart, 1)
    step = math.pi / width
    near = cotangent(apart.astype(F32) * step)
    far = cotangent((half - apart).astype(F32) * step)
    sign = jnp.where((column < half) == (apart % 2 == 0), 0.25 / width, -0.25 / width)
    sign = jnp.where(inside, sign, 0.0)
    tables = []
    for row in (sign * (near - far), sign * (near + far)):
        block = jnp.concatenate([row] * (half // 8), axis=0)
        tables.append(pltpu.roll(block, 0, 1, stride=1, stride_axis=0)[:, :half])
    return tables


def dot(a, b):
    return jnp.dot(a, b, preferred_element_type=F32)


def split(x):
    high = x.astype(BF16)
    return high, (x - high.astype(F32)).astype(BF16)


def derive(field, tables):
    half = field.shape[1] // 2
    left, right = field[:, :half], field[:, half:]
    sum_high, sum_low = split(left + right)
    gap_high, gap_low = split(left - right)
    even = dot(sum_high, tables[0]) + dot(sum_low, tables[0]) + dot(sum_high, tables[1])
    odd = dot(gap_high, tables[2]) + dot(gap_low, tables[2]) + dot(gap_high, tables[3])
    return jnp.concatenate([even + odd, even - odd], axis=1)


def mix(matrix, field):
    high, low = split(field)
    return dot(matrix[0], high) + dot(matrix[1], high) + dot(matrix[0], low)


def lanes(product):
    row = jnp.sum(product, axis=0, keepdims=True)
    return sum(row[:, k : k + 128] for k in range(0, row.shape[1], 128))


def total(row):
    return jnp.sum(row, axis=1, keepdims=True)


def kernel(
    groups, advect_in, growth_in, forcing_in, weight_in, flow_in, helm_in,
    mult_out, res_out, sens_out,
    advect, growth, forcing, weight, flow, helm, tables, matrix,
    state, other, p0, w0, y0, s1, w1, tang_flow, grad,
    flow_next, p_prev, w0_next, y_prev, w1_next,
    near_own, near_next, plane, line, line_next, coef,
    load_sem, send_sem, recv_sem,
    near_send, near_recv, next_recv, plane_send, plane_recv, line_send, line_recv, line_next_sem,
):
    seg_count, space_count, rows = groups
    seg, space = lax.axis_index("seg"), lax.axis_index("space")
    after, before = lax.rem(seg + 1, seg_count), lax.rem(seg + seg_count - 1, seg_count)
    steps, height, width = advect.shape
    planes = seg_count // rows
    active = jnp.where(seg < seg_count - 1, 1.0, 0.0).astype(F32)
    not_first = jnp.where(seg > 0, 1.0, 0.0).astype(F32)

    def load(slot, source, target):
        return pltpu.make_async_copy(source, target, load_sem.at[slot])

    def load_forcing(n):
        return load(n, forcing_in.at[n], forcing.at[n])

    def step_loads(n):
        return (
            load(steps + n, advect_in.at[n], advect.at[n]),
            load(2 * steps + n, growth_in.at[n], growth.at[n]),
        )

    base = 3 * steps
    load_helm = load(base, helm_in, helm)
    load_flow = load(base + 1, flow_in, flow)
    load_weight = load(base + 2, weight_in, weight)
    load_helm.start()
    load_forcing(0).start()
    for n in range(1, steps):
        for copy in (load_forcing(n), *step_loads(n)):
            copy.start()
    for copy in step_loads(0):
        copy.start()
    load_flow.start()
    load_weight.start()

    plane_me = (seg // rows) * space_count + space
    line_me = lax.rem(seg, rows)
    plane_size, line_size = planes * space_count, rows

    def plane_peer(d):
        j = lax.rem(plane_me + d, plane_size)
        return j, (lax.div(j, space_count) * rows + line_me, lax.rem(j, space_count))

    def line_peer(d):
        j = lax.rem(line_me + d, line_size)
        return j, ((seg // rows) * rows + j, space)

    barrier = pltpu.get_barrier_semaphore()
    greeted = [plane_peer(d)[1] for d in range(1, plane_size)]
    greeted += [line_peer(d)[1] for d in range(1, line_size)]
    greeted += [(s, lax.rem(space + d, space_count)) for s in (before, after) for d in range(space_count)]
    for peer in greeted:
        pl.semaphore_signal(barrier, inc=1, device_id=peer, device_id_type=MESH)

    piece = height // CHUNKS

    def transfer(kind, source, target, seg_to):
        return [
            pltpu.make_async_remote_copy(
                src_ref=source.at[pl.ds(c * piece, piece), :],
                dst_ref=target.at[pl.ds(c * piece, piece), :],
                send_sem=send_sem.at[kind, c],
                recv_sem=recv_sem.at[kind, c],
                device_id=(seg_to, space),
                device_id_type=MESH,
            )
            for c in range(CHUNKS)
        ]

    def start(copies):
        for copy in copies:
            copy.start()

    def arrived(copies):
        for copy in copies:
            copy.wait_recv()

    send_flow = transfer(0, flow_in, flow_next, before)
    send_p0 = transfer(1, p0, p_prev, after)
    send_w0 = transfer(2, w0, w0_next, before)
    send_y0 = transfer(3, y0, y_prev, after)
    send_w1 = transfer(4, w1, w1_next, before)

    def forward():
        return matrix[0], matrix[1]

    def backward():
        return matrix[2], matrix[3]

    def tangent(n, now, forced=False):
        rate = growth[n].astype(F32)
        speed = advect[n].astype(F32)
        update = now + rate * now - speed * derive(now, [tables[k] for k in range(4)])
        if forced:
            update = update + forcing[n].astype(F32)
        return mix(forward(), update)

    def adjoint_rest(n, pulled):
        rate = growth[n].astype(F32)
        speed = advect[n].astype(F32)
        return pulled + rate * pulled + derive(speed * pulled, [tables[k] for k in range(4)])

    def tangent_sweep(first, last):
        @pl.loop(first, last)
        def _(n):
            state[...] = tangent(n, state[...])

    def adjoint_sweep():
        @pl.loop(0, steps)
        def _(k):
            state[...] = adjoint_rest(steps - 1 - k, mix(backward(), state[...]))

    def gradient_step(k, now, flux):
        n = steps - 1 - k
        pulled = mix(backward(), weight[n].astype(F32) + now)
        return adjoint_rest(n, pulled), flux + lanes(pulled * forcing[n].astype(F32))

    def put(row, value):
        plane[plane_me, pl.ds(row, 1), :] = value

    for k, table in enumerate(derivative_tables(width)):
        tables[2 * k], tables[2 * k + 1] = split(table)

    load_helm.wait()
    high, low = split(helm[...])
    matrix[0], matrix[1] = high, low
    load_forcing(0).wait()
    state[...] = dot(matrix[0], forcing[0]) + dot(matrix[1], forcing[0])
    high, low = split(helm[...].T)
    matrix[2], matrix[3] = high, low
    pl.semaphore_wait(barrier, len(greeted))
    start(send_flow)

    @pl.loop(1, steps)
    def _(n):
        for copy in (load_forcing(n), *step_loads(n)):
            copy.wait()
        state[...] = tangent(n, state[...], forced=True)

    for c in range(CHUNKS):
        part = pl.ds(c * piece, piece)
        p0[part, :] = -active * state[part, :]
        send_p0[c].start()

    for copy in step_loads(0):
        copy.wait()
    state[...] = p0[...]
    adjoint_sweep()
    w0[...] = state[...]
    start(send_w0)
    load_flow.wait()
    load_weight.wait()
    put(0, lanes(flow[...] * flow[...]))
    put(8, lanes(p0[...] * p0[...]))
    plane[plane_me, pl.ds(11, 5), :] = jnp.zeros((5, 128), F32)

    def near_pairs():
        pairs = []
        for d in range(2 * space_count):
            own = d < space_count
            if d == 0:
                continue
            j = lax.rem(space + d, space_count)
            kept, sems = (near_own, near_recv) if own else (near_next, next_recv)
            to = (seg if own else before, j)
            pairs.append(
                (
                    pltpu.make_async_remote_copy(
                        src_ref=near_own.at[space], dst_ref=kept.at[space], send_sem=near_send.at[d - 1],
                        recv_sem=sems.at[space], device_id=to, device_id_type=MESH,
                    ),
                    pltpu.make_async_remote_copy(
                        src_ref=near_own.at[space], dst_ref=kept.at[j], send_sem=near_send.at[d - 1],
                        recv_sem=sems.at[j], device_id=to, device_id_type=MESH,
                    ),
                )
            )
        return pairs

    near_copies = near_pairs()

    def near_ratio(row, kept):
        sums = kept[0]
        for x in range(1, space_count):
            sums = sums + kept[x]
        c = total(sums[1:2]) / (total(sums[0:1]) + EPS)
        coef[pl.ds(row, 1), :] = jnp.broadcast_to(c, (1, 128))

    def begin_v0():
        arrived(send_p0)
        state[...] = w0[...] - p_prev[...]
        row = lanes(flow[...] * state[...])
        put(2, row)
        near_own[space] = jnp.concatenate(
            [plane[plane_me, pl.ds(0, 1), :], row, jnp.zeros((6, 128), F32)], axis=0
        )
        for copy, _ in near_copies:
            copy.start()
        put(3, lanes(state[...] * state[...]))

    def end_y0():
        for _, copy in near_copies[: space_count - 1]:
            copy.wait_recv()
        near_ratio(0, near_own)
        c0 = coef[0:1, 0:1]
        for c in range(CHUNKS):
            part = pl.ds(c * piece, piece)
            y0[part, :] = state[part, :] - c0 * tang_flow[part, :]
            send_y0[c].start()

    second = lax.rem(seg, 2) == 1

    @pl.when(second)
    def _():
        begin_v0()
        other[...] = flow[...]

        @pl.loop(0, steps)
        def _(n):
            one, two = tangent(n, state[...]), tangent(n, other[...])
            state[...] = one
            other[...] = two

        tang_flow[...] = other[...]
        end_y0()
        other[...] = jnp.zeros_like(other)

        def body(k, flux):
            now, flux = gradient_step(k, other[...], flux)
            other[...] = now
            return flux

        put(10, lax.fori_loop(0, steps, body, jnp.zeros((1, 128), F32)))
        grad[...] = other[...]

    @pl.when(jnp.logical_not(second))
    def _():
        other[...] = flow[...]
        state[...] = jnp.zeros_like(state)

        def body(k, flux):
            one = tangent(k, other[...])
            now, flux = gradient_step(k, state[...], flux)
            other[...] = one
            state[...] = now
            return flux

        put(10, lax.fori_loop(0, steps, body, jnp.zeros((1, 128), F32)))
        tang_flow[...] = other[...]
        grad[...] = state[...]
        begin_v0()
        tangent_sweep(0, steps)
        end_y0()

    put(1, lanes(grad[...] * flow[...]))
    put(4, lanes(grad[...] * (w0[...] - p_prev[...])))

    for _, copy in near_copies[space_count - 1 :]:
        copy.wait_recv()
    near_ratio(1, near_next)
    c0, c0_next = coef[0:1, 0:1], coef[1:2, 0:1]
    arrived(send_flow)
    arrived(send_w0)
    s1[...] = active * (2.0 * p0[...] + y0[...] - w0_next[...] + c0_next * flow_next[...])
    state[...] = s1[...]
    adjoint_sweep()
    w1[...] = state[...]
    start(send_w1)
    put(9, lanes(s1[...] * s1[...]))

    arrived(send_y0)
    state[...] = w1[...] - not_first * (2.0 * p_prev[...] + y_prev[...] - w0[...] + c0 * flow[...])
    for row, factor in ((5, flow), (6, state), (7, grad)):
        put(row, lanes(factor[...] * state[...]))

    def plane_copy(d):
        j, peer = plane_peer(d)
        send = pltpu.make_async_remote_copy(
            src_ref=plane.at[plane_me], dst_ref=plane.at[plane_me], send_sem=plane_send.at[d],
            recv_sem=plane_recv.at[plane_me], device_id=peer, device_id_type=MESH,
        )
        receive = pltpu.make_async_remote_copy(
            src_ref=plane.at[j], dst_ref=plane.at[j], send_sem=plane_send.at[d],
            recv_sem=plane_recv.at[j], device_id=peer, device_id_type=MESH,
        )
        return send, receive

    plane_copies = [plane_copy(d) for d in range(1, plane_size)]
    for copy, _ in plane_copies:
        copy.start()
    tangent_sweep(0, steps - 1)
    for _, copy in plane_copies:
        copy.wait_recv()

    def group_sums(k):
        tile = plane[k * space_count]
        for x in range(1, space_count):
            tile = tile + plane[k * space_count + x]
        return jnp.sum(tile, axis=1, keepdims=True)

    def group_terms(k):
        s = group_sums(k)
        norm, gf, fv0, vv0, gv0, fv1, vv1, gv1, pp, ss, flux = [s[r : r + 1] for r in range(11)]
        norm = norm + EPS
        a, b = fv0 / norm, fv1 / norm
        return [pp, vv0 - a * fv0, gv0 - a * gf, ss, vv1 - b * fv1, gv1 - b * gf, flux, b]

    terms = [group_terms(k) for k in range(planes)]
    summed = [sum(t[r] for t in terms[1:]) + terms[0][r] for r in range(7)]
    c1 = group_terms(seg // rows)[7]
    line[line_me] = jnp.concatenate([jnp.broadcast_to(t, (1, 128)) for t in [*summed, c1]], axis=0)

    def line_copy(d):
        j, peer = line_peer(d)
        send = pltpu.make_async_remote_copy(
            src_ref=line.at[line_me], dst_ref=line.at[line_me], send_sem=line_send.at[d],
            recv_sem=line_recv.at[line_me], device_id=peer, device_id_type=MESH,
        )
        receive = pltpu.make_async_remote_copy(
            src_ref=line.at[j], dst_ref=line.at[j], send_sem=line_send.at[d],
            recv_sem=line_recv.at[j], device_id=peer, device_id_type=MESH,
        )
        return send, receive

    line_copies = [line_copy(d) for d in range(1, line_size)]
    to_before = pltpu.make_async_remote_copy(
        src_ref=line.at[line_me], dst_ref=line_next, send_sem=line_send.at[0],
        recv_sem=line_next_sem, device_id=(before, space), device_id_type=MESH,
    )
    to_before.start()
    for copy, _ in line_copies:
        copy.start()
    tangent_sweep(steps - 1, steps)
    for _, copy in line_copies:
        copy.wait_recv()
    to_before.wait_recv()

    whole = line[0]
    for k in range(1, line_size):
        whole = whole + line[k]
    rr, q0, g0, m11, q1, g1, flux = [whole[r : r + 1, 0:1] for r in range(7)]
    c1_next = line_next[7:8, 0:1]
    k0 = rr + q0
    k11 = m11 + q1
    alpha0 = rr / k0
    fresh = alpha0 * alpha0 * m11 - rr
    beta = fresh / rr
    more = 1.0 + beta
    alpha1 = fresh / (more * more * k0 - 2.0 * alpha0 * more * m11 + alpha0 * alpha0 * k11)
    sens = flux + alpha0 * g0 + alpha1 * (more * g0 - alpha0 * g1)
    sens_out[...] = jnp.broadcast_to(sens, sens_out.shape)

    mult_out[...] = (alpha0 + alpha1 * more) * p0[...] - (alpha1 * alpha0) * s1[...]
    arrived(send_w1)
    s2 = 2.0 * s1[...] + state[...] - c1 * tang_flow[...] - w1_next[...] + c1_next * flow_next[...]
    res_out[...] = active * (
        p0[...] - (alpha0 + alpha1 * more) * s1[...] + (alpha1 * alpha0) * s2
    )

    for copies in (send_flow, send_p0, send_w0, send_y0, send_w1):
        for copy in copies:
            copy.wait_send()
    for copy, _ in near_copies + plane_copies + line_copies:
        copy.wait_send()
    to_before.wait_send()


def hand_over(mult_in, res_in, sens_in, mult_out, res_out, sens_out, sems):
    copies = [
        pltpu.make_async_copy(mult_in, mult_out, sems.at[0]),
        pltpu.make_async_copy(res_in, res_out, sems.at[1]),
    ]
    for copy in copies:
        copy.start()
    sens_out[...] = sens_in[0:1, 0:1]
    for copy in copies:
        copy.wait()


def on_device(rows, axes, advect, growth, forcing, flux_weight, flow_dir, helmholtz):
    steps, height, width = advect.shape[1], advect.shape[3], advect.shape[4]
    seg_count, space_count = axes
    planes = seg_count // rows
    plane_size = planes * space_count
    field = pltpu.VMEM((height, width), F32)
    steps_bf16 = pltpu.VMEM((steps, height, width), BF16)
    half = width // 2
    dma = pltpu.SemaphoreType.DMA
    shape = (steps, height, width)
    results = pl.pallas_call(
        functools.partial(kernel, (seg_count, space_count, rows)),
        out_shape=(
            pltpu.VMEM((height, width), F32),
            pltpu.VMEM((height, width), F32),
            pltpu.VMEM((8, 128), F32),
        ),
        in_specs=[pl.BlockSpec(memory_space=pl.ANY)] * 6,
        out_specs=tuple([pl.BlockSpec(memory_space=pltpu.VMEM)] * 3),
        scratch_shapes=[
            steps_bf16, steps_bf16, steps_bf16, steps_bf16, field,
            pltpu.VMEM((height, height), F32), pltpu.VMEM((4, half, half), BF16),
            pltpu.VMEM((4, height, height), BF16),
            *[field] * 9,
            *[field] * 5,
            pltpu.VMEM((space_count, 8, 128), F32), pltpu.VMEM((space_count, 8, 128), F32),
            pltpu.VMEM((plane_size, 16, 128), F32), pltpu.VMEM((rows, 8, 128), F32), pltpu.VMEM((8, 128), F32), pltpu.VMEM((8, 128), F32),
            dma((3 * steps + 3,)), dma((5, CHUNKS)), dma((5, CHUNKS)),
            dma((2 * space_count - 1,)), dma((space_count,)), dma((space_count,)),
            dma((plane_size,)), dma((plane_size,)), dma((rows,)), dma((rows,)), dma,
        ],
        compiler_params=pltpu.CompilerParams(
            collective_id=0, has_side_effects=True, vmem_limit_bytes=60 << 20
        ),
        cost_estimate=pl.CostEstimate(flops=8_000_000_000, bytes_accessed=6_000_000, transcendentals=0),
    )(
        advect.reshape(shape), growth.reshape(shape), forcing.reshape(shape), flux_weight.reshape(shape),
        flow_dir.reshape(height, width), helmholtz.reshape(height, height),
    )
    mult, res, sens = pl.pallas_call(
        hand_over,
        out_shape=(
            jax.ShapeDtypeStruct((height, width), F32),
            jax.ShapeDtypeStruct((height, width), F32),
            jax.ShapeDtypeStruct((1, 1), F32),
        ),
        in_specs=[pl.BlockSpec(memory_space=pl.ANY)] * 2 + [pl.BlockSpec(memory_space=pltpu.VMEM)],
        out_specs=(pl.BlockSpec(memory_space=pl.ANY),) * 2 + (pl.BlockSpec(memory_space=pltpu.VMEM),),
        scratch_shapes=[dma((2,))],
        compiler_params=pltpu.CompilerParams(vmem_limit_bytes=1 << 20),
    )(*results)
    return mult[None, None], res[None, None], sens.reshape(())


def solution(mesh):
    in_specs = (
        P("seg", None, "space", None, None),
        P("seg", None, "space", None, None),
        P("seg", None, "space", None, None),
        P("seg", None, "space", None, None),
        P("seg", "space", None, None),
        P("space", None, None),
    )
    out_specs = (P("seg", "space", None, None), P("seg", "space", None, None), P())
    axes = (mesh.shape["seg"], mesh.shape["space"])
    rows = 16 if axes[0] % 16 == 0 else axes[0]
    return jax.shard_map(
        functools.partial(on_device, rows, axes), mesh=mesh, in_specs=in_specs, out_specs=out_specs, check_vma=False
    )
```

```python
import functools
import math

import jax
import jax.numpy as jnp
from jax import lax
from jax.experimental import pallas as pl
from jax.experimental.pallas import tpu as pltpu
from jax.sharding import PartitionSpec as P

EPS = 1e-06
F32 = jnp.float32
BF16 = jnp.bfloat16
MESH = pl.DeviceIdType.MESH
CHUNKS = 4


def cotangent(angle):
    square = angle * angle
    sine = jnp.ones_like(angle)
    for n in (13, 11, 9, 7, 5, 3):
        sine = 1.0 - square * sine * (1.0 / (n * (n - 1)))
    cosine = jnp.ones_like(angle)
    for n in (14, 12, 10, 8, 6, 4, 2):
        cosine = 1.0 - square * cosine * (1.0 / (n * (n - 1)))
    return cosine / (angle * sine)


def derivative_tables(width):
    half = width // 2
    column = lax.broadcasted_iota(jnp.int32, (8, width), 1)
    apart = jnp.where(column < half, column, width - column)
    inside = jnp.logical_and(apart > 0, apart < half)
    apart = jnp.where(inside, apart, 1)
    step = math.pi / width
    near = cotangent(apart.astype(F32) * step)
    far = cotangent((half - apart).astype(F32) * step)
    sign = jnp.where((column < half) == (apart % 2 == 0), 0.25 / width, -0.25 / width)
    sign = jnp.where(inside, sign, 0.0)
    tables = []
    for row in (sign * (near - far), sign * (near + far)):
        block = jnp.concatenate([row] * (half // 8), axis=0)
        tables.append(pltpu.roll(block, 0, 1, stride=1, stride_axis=0)[:, :half])
    return tables


def dot(a, b):
    return jnp.dot(a, b, preferred_element_type=F32)


def split(x):
    high = x.astype(BF16)
    return high, (x - high.astype(F32)).astype(BF16)


def derive(field, tables):
    half = field.shape[1] // 2
    left, right = field[:, :half], field[:, half:]
    sum_high, sum_low = split(left + right)
    gap_high, gap_low = split(left - right)
    even = dot(sum_high, tables[0]) + dot(sum_low, tables[0]) + dot(sum_high, tables[1])
    odd = dot(gap_high, tables[2]) + dot(gap_low, tables[2]) + dot(gap_high, tables[3])
    return jnp.concatenate([even + odd, even - odd], axis=1)


def mix(matrix, field):
    high, low = split(field)
    return dot(matrix[0], high) + dot(matrix[1], high) + dot(matrix[0], low)


def lanes(product):
    row = jnp.sum(product, axis=0, keepdims=True)
    return sum(row[:, k : k + 128] for k in range(0, row.shape[1], 128))


def total(row):
    return jnp.sum(row, axis=1, keepdims=True)


def kernel(
    groups, advect_in, growth_in, forcing_in, weight_in, flow_in, helm_in,
    mult_out, res_out, sens_out,
    advect, growth, forcing, weight, helm, tables, matrix,
    from_p0, from_s1, from_flow, from_v, from_weight, y0,
    flow_next, p_prev, w0_next, y_prev, w1_next,
    near_own, near_next, plane, line, line_next, coef,
    load_sem, send_sem, recv_sem,
    near_send, near_recv, next_recv, plane_send, plane_recv, line_send, line_recv, line_next_sem,
):
    seg_count, space_count, rows = groups
    seg, space = lax.axis_index("seg"), lax.axis_index("space")
    after, before = lax.rem(seg + 1, seg_count), lax.rem(seg + seg_count - 1, seg_count)
    steps, height, width = advect.shape
    planes = seg_count // rows
    active = jnp.where(seg < seg_count - 1, 1.0, 0.0).astype(F32)
    not_first = jnp.where(seg > 0, 1.0, 0.0).astype(F32)

    def load(slot, source, target):
        return pltpu.make_async_copy(source, target, load_sem.at[slot])

    def load_forcing(n):
        return load(n, forcing_in.at[n], forcing.at[n])

    def step_loads(n):
        return (
            load(steps + n, advect_in.at[n], advect.at[n]),
            load(2 * steps + n, growth_in.at[n], growth.at[n]),
        )

    p0, w0 = from_p0.at[0], from_p0.at[steps]
    s1, w1 = from_s1.at[0], from_s1.at[steps]
    flow, grad = from_flow.at[0], from_weight.at[steps]
    v = from_v.at[0]

    base = 3 * steps
    load_helm = load(base, helm_in, helm)
    load_flow = load(base + 1, flow_in, flow)
    load_weight = load(base + 2, weight_in, weight)
    load_helm.start()
    load_forcing(0).start()
    for n in range(1, steps):
        for copy in (load_forcing(n), *step_loads(n)):
            copy.start()
    for copy in step_loads(0):
        copy.start()
    load_flow.start()
    load_weight.start()

    plane_me = (seg // rows) * space_count + space
    line_me = lax.rem(seg, rows)
    plane_size, line_size = planes * space_count, rows

    def ring(distance, size):
        return min(distance, size - distance)

    def offsets(first, second):
        pairs = [(a, b) for a in range(first) for b in range(second)][1:]
        return sorted(pairs, key=lambda pair: -ring(pair[0], first) - ring(pair[1], second))

    plane_shifts = offsets(planes, space_count)
    line_shifts = offsets(rows // 2, 2)

    def plane_peer(shift):
        plane_at = lax.rem(lax.div(seg, rows) + shift[0], planes)
        x = lax.rem(space + shift[1], space_count)
        return plane_at * space_count + x, (plane_at * rows + line_me, x)

    def line_peer(shift):
        chip = lax.rem(lax.div(line_me, 2) + shift[0], rows // 2)
        j = chip * 2 + lax.rem(lax.rem(line_me, 2) + shift[1], 2)
        return j, (lax.div(seg, rows) * rows + j, space)

    barrier = pltpu.get_barrier_semaphore()
    greeted = [plane_peer(shift)[1] for shift in plane_shifts]
    greeted += [line_peer(shift)[1] for shift in line_shifts]
    greeted += [(s, lax.rem(space + d, space_count)) for s in (before, after) for d in range(space_count)]
    for peer in greeted:
        pl.semaphore_signal(barrier, inc=1, device_id=peer, device_id_type=MESH)

    piece = height // CHUNKS

    def transfer(kind, source, target, seg_to):
        return [
            pltpu.make_async_remote_copy(
                src_ref=source.at[pl.ds(c * piece, piece), :],
                dst_ref=target.at[pl.ds(c * piece, piece), :],
                send_sem=send_sem.at[kind, c],
                recv_sem=recv_sem.at[kind, c],
                device_id=(seg_to, space),
                device_id_type=MESH,
            )
            for c in range(CHUNKS)
        ]

    parts = [pl.ds(c * piece, piece) for c in range(CHUNKS)]

    def start(copies):
        for copy in copies:
            copy.start()

    def arrived(copies):
        for copy in copies:
            copy.wait_recv()

    send_flow = transfer(0, flow_in, flow_next, before)
    send_p0 = transfer(1, p0, p_prev, after)
    send_w0 = transfer(2, w0, w0_next, before)
    send_y0 = transfer(3, y0, y_prev, after)
    send_w1 = transfer(4, w1, w1_next, before)

    def forward():
        return matrix[0], matrix[1]

    def backward():
        return matrix[2], matrix[3]

    def tangent(n, now, forced=False):
        rate = growth[n].astype(F32)
        speed = advect[n].astype(F32)
        update = now + rate * now - speed * derive(now, [tables[k] for k in range(4)])
        if forced:
            update = update + forcing[n].astype(F32)
        return mix(forward(), update)

    def adjoint_rest(n, pulled):
        rate = growth[n].astype(F32)
        speed = advect[n].astype(F32)
        return pulled + rate * pulled + derive(speed * pulled, [tables[k] for k in range(4)])

    def tangent_sweep(path, first, last):
        @pl.loop(first, last)
        def _(n):
            path[n + 1] = tangent(n, path[n])

    def adjoint_sweep(path):
        @pl.loop(0, steps)
        def _(k):
            path[k + 1] = adjoint_rest(steps - 1 - k, mix(backward(), path[k]))

    def gradient_step(k, flux):
        n = steps - 1 - k
        pulled = mix(backward(), weight[n].astype(F32) + from_weight[k])
        return adjoint_rest(n, pulled), flux + lanes(pulled * forcing[n].astype(F32))

    def put(row, value):
        plane[plane_me, pl.ds(row, 1), :] = value

    for k, table in enumerate(derivative_tables(width)):
        tables[2 * k], tables[2 * k + 1] = split(table)

    load_helm.wait()
    high, low = split(helm[...])
    matrix[0], matrix[1] = high, low
    load_forcing(0).wait()
    from_v[1] = dot(matrix[0], forcing[0]) + dot(matrix[1], forcing[0])
    high, low = split(helm[...].T)
    matrix[2], matrix[3] = high, low
    pl.semaphore_wait(barrier, len(greeted))
    start(send_flow)

    @pl.loop(1, steps)
    def _(n):
        for copy in (load_forcing(n), *step_loads(n)):
            copy.wait()
        from_v[n + 1] = tangent(n, from_v[n], forced=True)

    for part, copy in zip(parts, send_p0):
        p0[part, :] = -active * from_v[steps, part, :]
        copy.start()

    for copy in step_loads(0):
        copy.wait()
    adjoint_sweep(from_p0)
    start(send_w0)
    load_flow.wait()
    load_weight.wait()
    from_weight[0] = jnp.zeros_like(from_weight[0])
    put(0, lanes(flow[...] * flow[...]))
    put(8, lanes(p0[...] * p0[...]))
    plane[plane_me, pl.ds(11, 5), :] = jnp.zeros((5, 128), F32)

    def near_pairs():
        pairs = []
        for d in range(1, 2 * space_count):
            own = d < space_count
            j = lax.rem(space + d, space_count)
            kept, sems = (near_own, near_recv) if own else (near_next, next_recv)
            to = (seg if own else before, j)
            pairs.append(
                (
                    pltpu.make_async_remote_copy(
                        src_ref=near_own.at[space], dst_ref=kept.at[space], send_sem=near_send.at[d - 1],
                        recv_sem=sems.at[space], device_id=to, device_id_type=MESH,
                    ),
                    pltpu.make_async_remote_copy(
                        src_ref=near_own.at[space], dst_ref=kept.at[j], send_sem=near_send.at[d - 1],
                        recv_sem=sems.at[j], device_id=to, device_id_type=MESH,
                    ),
                )
            )
        return pairs

    near_copies = near_pairs()

    def near_ratio(row, kept):
        sums = kept[0]
        for x in range(1, space_count):
            sums = sums + kept[x]
        c = total(sums[1:2]) / (total(sums[0:1]) + EPS)
        coef[pl.ds(row, 1), :] = jnp.broadcast_to(c, (1, 128))

    def begin_v0():
        row = jnp.zeros((1, 128), F32)
        for part, copy in zip(parts, send_p0):
            copy.wait_recv()
            piece_of = w0[part, :] - p_prev[part, :]
            v[part, :] = piece_of
            row = row + lanes(flow[part, :] * piece_of)
        put(2, row)
        near_own[space] = jnp.concatenate(
            [plane[plane_me, pl.ds(0, 1), :], row, jnp.zeros((6, 128), F32)], axis=0
        )
        for copy, _ in near_copies:
            copy.start()
        put(3, lanes(v[...] * v[...]))

    def own_ratio():
        for _, copy in near_copies[: space_count - 1]:
            copy.wait_recv()
        near_ratio(0, near_own)
        return coef[0:1, 0:1]

    second = lax.rem(seg, 2) == 1

    @pl.when(second)
    def _():
        begin_v0()

        @pl.loop(0, steps - 1)
        def _(n):
            one, two = tangent(n, from_v[n]), tangent(n, from_flow[n])
            from_v[n + 1] = one
            from_flow[n + 1] = two

        y0[...] = tangent(steps - 1, from_v[steps - 1] - own_ratio() * from_flow[steps - 1])
        start(send_y0)

        def body(k, flux):
            now, flux = gradient_step(k, flux)
            from_weight[k + 1] = now
            return flux

        put(10, lax.fori_loop(0, steps, body, jnp.zeros((1, 128), F32)))

    @pl.when(jnp.logical_not(second))
    def _():
        def body(k, flux):
            one = tangent(k, from_flow[k])
            now, flux = gradient_step(k, flux)
            from_flow[k + 1] = one
            from_weight[k + 1] = now
            return flux

        put(10, lax.fori_loop(0, steps, body, jnp.zeros((1, 128), F32)))
        begin_v0()
        tangent_sweep(from_v, 0, steps)
        c0 = own_ratio()
        for part, copy in zip(parts, send_y0):
            y0[part, :] = from_v[steps, part, :] - c0 * from_flow[steps, part, :]
            copy.start()

    put(1, lanes(grad[...] * flow[...]))
    put(4, lanes(grad[...] * v[...]))

    for _, copy in near_copies[space_count - 1 :]:
        copy.wait_recv()
    near_ratio(1, near_next)
    c0, c0_next = coef[0:1, 0:1], coef[1:2, 0:1]
    arrived(send_flow)
    row = jnp.zeros((1, 128), F32)
    for part, copy in zip(parts, send_w0):
        copy.wait_recv()
        piece_of = active * (
            2.0 * p0[part, :] + y0[part, :] - w0_next[part, :] + c0_next * flow_next[part, :]
        )
        s1[part, :] = piece_of
        row = row + lanes(piece_of * piece_of)
    put(9, row)
    adjoint_sweep(from_s1)
    start(send_w1)

    v1_rows = [jnp.zeros((1, 128), F32)] * 3
    for part, copy in zip(parts, send_y0):
        copy.wait_recv()
        piece_of = w1[part, :] - not_first * (
            2.0 * p_prev[part, :] + y_prev[part, :] - w0[part, :] + c0 * flow[part, :]
        )
        v[part, :] = piece_of
        factors = (flow[part, :], piece_of, grad[part, :])
        v1_rows = [row + lanes(factor * piece_of) for row, factor in zip(v1_rows, factors)]
    plane[plane_me, pl.ds(5, 3), :] = jnp.concatenate(v1_rows, axis=0)

    def plane_copy(d, shift):
        j, peer = plane_peer(shift)
        send = pltpu.make_async_remote_copy(
            src_ref=plane.at[plane_me], dst_ref=plane.at[plane_me], send_sem=plane_send.at[d],
            recv_sem=plane_recv.at[plane_me], device_id=peer, device_id_type=MESH,
        )
        receive = pltpu.make_async_remote_copy(
            src_ref=plane.at[j], dst_ref=plane.at[j], send_sem=plane_send.at[d],
            recv_sem=plane_recv.at[j], device_id=peer, device_id_type=MESH,
        )
        return send, receive

    plane_copies = [plane_copy(d, shift) for d, shift in enumerate(plane_shifts)]
    for copy, _ in plane_copies:
        copy.start()
    tangent_sweep(from_v, 0, steps - 1)
    for _, copy in plane_copies:
        copy.wait_recv()

    lane = lax.broadcasted_iota(jnp.int32, (16, 128), 1)
    sums = jnp.zeros((16, 128), F32)
    for k in range(planes):
        tile = plane[k * space_count]
        for x in range(1, space_count):
            tile = tile + plane[k * space_count + x]
        sums = jnp.where(lane == k, jnp.sum(tile, axis=1, keepdims=True), sums)
    norm, gf, fv0, vv0, gv0, fv1, vv1, gv1, pp, ss, flux = [sums[r : r + 1] for r in range(11)]
    norm = norm + EPS
    a, b = fv0 / norm, fv1 / norm
    mine = jnp.where(lane[0:1] == lax.div(seg, rows), b, 0.0)
    line[line_me] = jnp.concatenate(
        [pp, vv0 - a * fv0, gv0 - a * gf, ss, vv1 - b * fv1, gv1 - b * gf, flux, mine], axis=0
    )

    def line_copy(d, shift):
        j, peer = line_peer(shift)
        send = pltpu.make_async_remote_copy(
            src_ref=line.at[line_me], dst_ref=line.at[line_me], send_sem=line_send.at[d],
            recv_sem=line_recv.at[line_me], device_id=peer, device_id_type=MESH,
        )
        receive = pltpu.make_async_remote_copy(
            src_ref=line.at[j], dst_ref=line.at[j], send_sem=line_send.at[d],
            recv_sem=line_recv.at[j], device_id=peer, device_id_type=MESH,
        )
        return send, receive

    line_copies = [line_copy(d + 1, shift) for d, shift in enumerate(line_shifts)]
    to_before = pltpu.make_async_remote_copy(
        src_ref=line.at[line_me], dst_ref=line_next, send_sem=line_send.at[0],
        recv_sem=line_next_sem, device_id=(before, space), device_id_type=MESH,
    )
    to_before.start()
    for copy, _ in line_copies:
        copy.start()
    c1 = total(mine)
    from_v[steps] = tangent(steps - 1, from_v[steps - 1] - c1 * from_flow[steps - 1])
    to_before.wait_recv()
    c1_next = total(line_next[7:8])
    for _, copy in line_copies:
        copy.wait_recv()

    whole = line[0]
    for k in range(1, line_size):
        whole = whole + line[k]
    whole = jnp.sum(whole, axis=1, keepdims=True)
    rr, q0, g0, m11, q1, g1, flux = [whole[r : r + 1] for r in range(7)]
    k0 = rr + q0
    k11 = m11 + q1
    alpha0 = rr / k0
    fresh = alpha0 * alpha0 * m11 - rr
    beta = fresh / rr
    more = 1.0 + beta
    alpha1 = fresh / (more * more * k0 - 2.0 * alpha0 * more * m11 + alpha0 * alpha0 * k11)
    sens = flux + alpha0 * g0 + alpha1 * (more * g0 - alpha0 * g1)
    sens_out[...] = jnp.broadcast_to(sens, sens_out.shape)

    along, across = alpha0 + alpha1 * more, alpha1 * alpha0
    mult_out[...] = along * p0[...] - across * s1[...]
    for part, copy in zip(parts, send_w1):
        copy.wait_recv()
        s2 = 2.0 * s1[part, :] + from_v[steps, part, :] - w1_next[part, :] + c1_next * flow_next[part, :]
        res_out[part, :] = active * (p0[part, :] - along * s1[part, :] + across * s2)

    for copies in (send_flow, send_p0, send_w0, send_y0, send_w1):
        for copy in copies:
            copy.wait_send()
    for copy, _ in near_copies + plane_copies + line_copies:
        copy.wait_send()
    to_before.wait_send()


def hand_over(mult_in, res_in, sens_in, mult_out, res_out, sens_out, sems):
    copies = [
        pltpu.make_async_copy(mult_in, mult_out, sems.at[0]),
        pltpu.make_async_copy(res_in, res_out, sems.at[1]),
    ]
    for copy in copies:
        copy.start()
    sens_out[...] = sens_in[0:1, 0:1]
    for copy in copies:
        copy.wait()


def on_device(rows, axes, advect, growth, forcing, flux_weight, flow_dir, helmholtz):
    steps, height, width = advect.shape[1], advect.shape[3], advect.shape[4]
    seg_count, space_count = axes
    planes = seg_count // rows
    plane_size = planes * space_count
    field = pltpu.VMEM((height, width), F32)
    steps_bf16 = pltpu.VMEM((steps, height, width), BF16)
    half = width // 2
    dma = pltpu.SemaphoreType.DMA
    shape = (steps, height, width)
    results = pl.pallas_call(
        functools.partial(kernel, (seg_count, space_count, rows)),
        out_shape=(
            pltpu.VMEM((height, width), F32),
            pltpu.VMEM((height, width), F32),
            pltpu.VMEM((8, 128), F32),
        ),
        in_specs=[pl.BlockSpec(memory_space=pl.ANY)] * 6,
        out_specs=tuple([pl.BlockSpec(memory_space=pltpu.VMEM)] * 3),
        scratch_shapes=[
            steps_bf16, steps_bf16, steps_bf16, steps_bf16,
            pltpu.VMEM((height, height), F32), pltpu.VMEM((4, half, half), BF16),
            pltpu.VMEM((4, height, height), BF16),
            *[pltpu.VMEM((steps + 1, height, width), F32)] * 5, field,
            *[field] * 5,
            pltpu.VMEM((space_count, 8, 128), F32), pltpu.VMEM((space_count, 8, 128), F32),
            pltpu.VMEM((plane_size, 16, 128), F32), pltpu.VMEM((rows, 8, 128), F32), pltpu.VMEM((8, 128), F32), pltpu.VMEM((8, 128), F32),
            dma((3 * steps + 3,)), dma((5, CHUNKS)), dma((5, CHUNKS)),
            dma((2 * space_count - 1,)), dma((space_count,)), dma((space_count,)),
            dma((plane_size,)), dma((plane_size,)), dma((rows,)), dma((rows,)), dma,
        ],
        compiler_params=pltpu.CompilerParams(
            collective_id=0, has_side_effects=True, vmem_limit_bytes=60 << 20
        ),
        cost_estimate=pl.CostEstimate(flops=8_000_000_000, bytes_accessed=6_000_000, transcendentals=0),
    )(
        advect.reshape(shape), growth.reshape(shape), forcing.reshape(shape), flux_weight.reshape(shape),
        flow_dir.reshape(height, width), helmholtz.reshape(height, height),
    )
    mult, res, sens = pl.pallas_call(
        hand_over,
        out_shape=(
            jax.ShapeDtypeStruct((height, width), F32),
            jax.ShapeDtypeStruct((height, width), F32),
            jax.ShapeDtypeStruct((1, 1), F32),
        ),
        in_specs=[pl.BlockSpec(memory_space=pl.ANY)] * 2 + [pl.BlockSpec(memory_space=pltpu.VMEM)],
        out_specs=(pl.BlockSpec(memory_space=pl.ANY),) * 2 + (pl.BlockSpec(memory_space=pltpu.VMEM),),
        scratch_shapes=[dma((2,))],
        compiler_params=pltpu.CompilerParams(vmem_limit_bytes=1 << 20),
    )(*results)
    return mult[None, None], res[None, None], sens.reshape(())


def solution(mesh):
    in_specs = (
        P("seg", None, "space", None, None),
        P("seg", None, "space", None, None),
        P("seg", None, "space", None, None),
        P("seg", None, "space", None, None),
        P("seg", "space", None, None),
        P("space", None, None),
    )
    out_specs = (P("seg", "space", None, None), P("seg", "space", None, None), P())
    axes = (mesh.shape["seg"], mesh.shape["space"])
    rows = 16 if axes[0] % 16 == 0 else axes[0]
    return jax.shard_map(
        functools.partial(on_device, rows, axes), mesh=mesh, in_specs=in_specs, out_specs=out_specs, check_vma=False
    )
```

```python
import functools
import math

import jax
import jax.numpy as jnp
from jax import lax
from jax.experimental import pallas as pl
from jax.experimental.pallas import tpu as pltpu
from jax.sharding import PartitionSpec as P

EPS = 1e-06
F32 = jnp.float32
BF16 = jnp.bfloat16
MESH = pl.DeviceIdType.MESH
CHUNKS = 4


def cotangent(angle):
    square = angle * angle
    sine = jnp.ones_like(angle)
    for n in (13, 11, 9, 7, 5, 3):
        sine = 1.0 - square * sine * (1.0 / (n * (n - 1)))
    cosine = jnp.ones_like(angle)
    for n in (14, 12, 10, 8, 6, 4, 2):
        cosine = 1.0 - square * cosine * (1.0 / (n * (n - 1)))
    return cosine / (angle * sine)


def derivative_tables(width):
    half = width // 2
    column = lax.broadcasted_iota(jnp.int32, (8, width), 1)
    apart = jnp.where(column < half, column, width - column)
    inside = jnp.logical_and(apart > 0, apart < half)
    apart = jnp.where(inside, apart, 1)
    step = math.pi / width
    near = cotangent(apart.astype(F32) * step)
    far = cotangent((half - apart).astype(F32) * step)
    sign = jnp.where((column < half) == (apart % 2 == 0), 0.25 / width, -0.25 / width)
    sign = jnp.where(inside, sign, 0.0)
    tables = []
    for row in (sign * (near - far), sign * (near + far)):
        block = jnp.concatenate([row] * (half // 8), axis=0)
        tables.append(pltpu.roll(block, 0, 1, stride=1, stride_axis=0)[:, :half])
    return tables


def dot(a, b):
    return jnp.dot(a, b, preferred_element_type=F32)


def split(x):
    high = x.astype(BF16)
    return high, (x - high.astype(F32)).astype(BF16)


def derive(field, tables):
    half = field.shape[1] // 2
    left, right = field[:, :half], field[:, half:]
    sum_high, sum_low = split(left + right)
    gap_high, gap_low = split(left - right)
    even = dot(sum_high, tables[0]) + dot(sum_low, tables[0]) + dot(sum_high, tables[1])
    odd = dot(gap_high, tables[2]) + dot(gap_low, tables[2]) + dot(gap_high, tables[3])
    return jnp.concatenate([even + odd, even - odd], axis=1)


def mix(matrix, field):
    high, low = split(field)
    return dot(matrix[0], high) + dot(matrix[1], high) + dot(matrix[0], low)


def lanes(product):
    row = jnp.sum(product, axis=0, keepdims=True)
    return sum(row[:, k : k + 128] for k in range(0, row.shape[1], 128))


def total(row):
    return jnp.sum(row, axis=1, keepdims=True)


def kernel(
    groups, advect_in, growth_in, forcing_in, weight_in, flow_in, helm_in,
    p0_out, s1_out, s2_out, coef_out,
    advect, growth, forcing, weight, helm, tables, matrix,
    from_p0, from_s1, from_flow, from_v, from_weight, y0,
    flow_next, p_prev, w0_next, y_prev, w1_next,
    near_own, near_next, plane, line, line_next, coef,
    load_sem, send_sem, recv_sem,
    near_send, near_recv, next_recv, plane_send, plane_recv, line_send, line_recv, line_next_sem,
):
    seg_count, space_count, rows = groups
    seg, space = lax.axis_index("seg"), lax.axis_index("space")
    after, before = lax.rem(seg + 1, seg_count), lax.rem(seg + seg_count - 1, seg_count)
    steps, height, width = advect.shape
    planes = seg_count // rows
    active = jnp.where(seg < seg_count - 1, 1.0, 0.0).astype(F32)
    not_first = jnp.where(seg > 0, 1.0, 0.0).astype(F32)

    def load(slot, source, target):
        return pltpu.make_async_copy(source, target, load_sem.at[slot])

    def load_forcing(n):
        return load(n, forcing_in.at[n], forcing.at[n])

    def step_loads(n):
        return (
            load(steps + n, advect_in.at[n], advect.at[n]),
            load(2 * steps + n, growth_in.at[n], growth.at[n]),
        )

    p0, w0 = from_p0.at[0], from_p0.at[steps]
    s1, w1 = from_s1.at[0], from_s1.at[steps]
    flow, grad = from_flow.at[0], from_weight.at[steps]
    v = from_v.at[0]

    base = 3 * steps
    load_helm = load(base, helm_in, helm)
    load_flow = load(base + 1, flow_in, flow)
    load_weight = load(base + 2, weight_in, weight)
    load_helm.start()
    load_forcing(0).start()
    for n in range(1, steps):
        for copy in (load_forcing(n), *step_loads(n)):
            copy.start()
    for copy in step_loads(0):
        copy.start()
    load_flow.start()
    load_weight.start()

    plane_me = (seg // rows) * space_count + space
    line_me = lax.rem(seg, rows)
    plane_size, line_size = planes * space_count, rows

    def ring(distance, size):
        return min(distance, size - distance)

    def offsets(first, second):
        pairs = [(a, b) for a in range(first) for b in range(second)][1:]
        return sorted(pairs, key=lambda pair: -ring(pair[0], first) - ring(pair[1], second))

    plane_shifts = offsets(planes, space_count)
    line_shifts = offsets(rows // 2, 2)

    def plane_peer(shift):
        plane_at = lax.rem(lax.div(seg, rows) + shift[0], planes)
        x = lax.rem(space + shift[1], space_count)
        return plane_at * space_count + x, (plane_at * rows + line_me, x)

    def line_peer(shift):
        chip = lax.rem(lax.div(line_me, 2) + shift[0], rows // 2)
        j = chip * 2 + lax.rem(lax.rem(line_me, 2) + shift[1], 2)
        return j, (lax.div(seg, rows) * rows + j, space)

    barrier = pltpu.get_barrier_semaphore()
    greeted = [plane_peer(shift)[1] for shift in plane_shifts]
    greeted += [line_peer(shift)[1] for shift in line_shifts]
    greeted += [(s, lax.rem(space + d, space_count)) for s in (before, after) for d in range(space_count)]
    for peer in greeted:
        pl.semaphore_signal(barrier, inc=1, device_id=peer, device_id_type=MESH)

    piece = height // CHUNKS

    def transfer(kind, source, target, seg_to):
        return [
            pltpu.make_async_remote_copy(
                src_ref=source.at[pl.ds(c * piece, piece), :],
                dst_ref=target.at[pl.ds(c * piece, piece), :],
                send_sem=send_sem.at[kind, c],
                recv_sem=recv_sem.at[kind, c],
                device_id=(seg_to, space),
                device_id_type=MESH,
            )
            for c in range(CHUNKS)
        ]

    parts = [pl.ds(c * piece, piece) for c in range(CHUNKS)]

    def start(copies):
        for copy in copies:
            copy.start()

    def arrived(copies):
        for copy in copies:
            copy.wait_recv()

    send_flow = transfer(0, flow_in, flow_next, before)
    send_p0 = transfer(1, p0, p_prev, after)
    send_w0 = transfer(2, w0, w0_next, before)
    send_y0 = transfer(3, y0, y_prev, after)
    send_w1 = transfer(4, w1, w1_next, before)

    def forward():
        return matrix[0], matrix[1]

    def backward():
        return matrix[2], matrix[3]

    def tangent(n, now, forced=False):
        rate = growth[n].astype(F32)
        speed = advect[n].astype(F32)
        update = now + rate * now - speed * derive(now, [tables[k] for k in range(4)])
        if forced:
            update = update + forcing[n].astype(F32)
        return mix(forward(), update)

    def adjoint_rest(n, pulled):
        rate = growth[n].astype(F32)
        speed = advect[n].astype(F32)
        return pulled + rate * pulled + derive(speed * pulled, [tables[k] for k in range(4)])

    def tangent_sweep(path, first, last):
        @pl.loop(first, last)
        def _(n):
            path[n + 1] = tangent(n, path[n])

    def adjoint_sweep(path):
        @pl.loop(0, steps)
        def _(k):
            path[k + 1] = adjoint_rest(steps - 1 - k, mix(backward(), path[k]))

    def gradient_step(k, flux):
        n = steps - 1 - k
        pulled = mix(backward(), weight[n].astype(F32) + from_weight[k])
        return adjoint_rest(n, pulled), flux + lanes(pulled * forcing[n].astype(F32))

    def put(row, value):
        plane[plane_me, pl.ds(row, 1), :] = value

    for k, table in enumerate(derivative_tables(width)):
        tables[2 * k], tables[2 * k + 1] = split(table)

    load_helm.wait()
    high, low = split(helm[...])
    matrix[0], matrix[1] = high, low
    load_forcing(0).wait()
    from_v[1] = dot(matrix[0], forcing[0]) + dot(matrix[1], forcing[0])
    high, low = split(helm[...].T)
    matrix[2], matrix[3] = high, low
    pl.semaphore_wait(barrier, len(greeted))
    start(send_flow)

    @pl.loop(1, steps)
    def _(n):
        for copy in (load_forcing(n), *step_loads(n)):
            copy.wait()
        from_v[n + 1] = tangent(n, from_v[n], forced=True)

    for part, copy in zip(parts, send_p0):
        p0[part, :] = -active * from_v[steps, part, :]
        copy.start()

    for copy in step_loads(0):
        copy.wait()
    adjoint_sweep(from_p0)
    start(send_w0)
    load_flow.wait()
    load_weight.wait()
    from_weight[0] = jnp.zeros_like(from_weight[0])
    put(0, lanes(flow[...] * flow[...]))

    def near_pairs():
        pairs = []
        for d in range(1, 2 * space_count):
            own = d < space_count
            j = lax.rem(space + d, space_count)
            kept, sems = (near_own, near_recv) if own else (near_next, next_recv)
            to = (seg if own else before, j)
            pairs.append(
                (
                    pltpu.make_async_remote_copy(
                        src_ref=near_own.at[space], dst_ref=kept.at[space], send_sem=near_send.at[d - 1],
                        recv_sem=sems.at[space], device_id=to, device_id_type=MESH,
                    ),
                    pltpu.make_async_remote_copy(
                        src_ref=near_own.at[space], dst_ref=kept.at[j], send_sem=near_send.at[d - 1],
                        recv_sem=sems.at[j], device_id=to, device_id_type=MESH,
                    ),
                )
            )
        return pairs

    near_copies = near_pairs()

    def near_ratio(row, kept):
        sums = kept[0]
        for x in range(1, space_count):
            sums = sums + kept[x]
        c = total(sums[1:2]) / (total(sums[0:1]) + EPS)
        coef[pl.ds(row, 1), :] = jnp.broadcast_to(c, (1, 128))

    def begin_v0():
        row = jnp.zeros((1, 128), F32)
        for part, copy in zip(parts, send_p0):
            copy.wait_recv()
            piece_of = w0[part, :] - p_prev[part, :]
            v[part, :] = piece_of
            row = row + lanes(flow[part, :] * piece_of)
        put(2, row)
        near_own[space] = jnp.concatenate(
            [plane[plane_me, pl.ds(0, 1), :], row, jnp.zeros((6, 128), F32)], axis=0
        )
        for copy, _ in near_copies:
            copy.start()

    def v0_sums():
        put(1, lanes(grad[...] * flow[...]))
        put(3, lanes(v[...] * v[...]))
        put(4, lanes(grad[...] * v[...]))
        put(8, lanes(p0[...] * p0[...]))
        plane[plane_me, pl.ds(11, 5), :] = jnp.zeros((5, 128), F32)

    def own_ratio():
        for _, copy in near_copies[: space_count - 1]:
            copy.wait_recv()
        near_ratio(0, near_own)
        return coef[0:1, 0:1]

    second = lax.rem(seg, 2) == 1

    @pl.when(second)
    def _():
        begin_v0()

        @pl.loop(0, steps - 1)
        def _(n):
            one, two = tangent(n, from_v[n]), tangent(n, from_flow[n])
            from_v[n + 1] = one
            from_flow[n + 1] = two

        y0[...] = tangent(steps - 1, from_v[steps - 1] - own_ratio() * from_flow[steps - 1])
        start(send_y0)

        def body(k, flux):
            now, flux = gradient_step(k, flux)
            from_weight[k + 1] = now
            return flux

        put(10, lax.fori_loop(0, steps, body, jnp.zeros((1, 128), F32)))
        v0_sums()

    @pl.when(jnp.logical_not(second))
    def _():
        def body(k, flux):
            one = tangent(k, from_flow[k])
            now, flux = gradient_step(k, flux)
            from_flow[k + 1] = one
            from_weight[k + 1] = now
            return flux

        put(10, lax.fori_loop(0, steps, body, jnp.zeros((1, 128), F32)))
        begin_v0()
        tangent_sweep(from_v, 0, steps)
        v0_sums()
        c0 = own_ratio()
        for part, copy in zip(parts, send_y0):
            y0[part, :] = from_v[steps, part, :] - c0 * from_flow[steps, part, :]
            copy.start()

    for _, copy in near_copies[space_count - 1 :]:
        copy.wait_recv()
    near_ratio(1, near_next)
    c0, c0_next = coef[0:1, 0:1], coef[1:2, 0:1]
    arrived(send_flow)
    row = jnp.zeros((1, 128), F32)
    for part, copy in zip(parts, send_w0):
        copy.wait_recv()
        piece_of = active * (
            2.0 * p0[part, :] + y0[part, :] - w0_next[part, :] + c0_next * flow_next[part, :]
        )
        s1[part, :] = piece_of
        row = row + lanes(piece_of * piece_of)
    put(9, row)
    adjoint_sweep(from_s1)
    start(send_w1)
    p0_out[...] = p0[...]
    s1_out[...] = s1[...]

    v1_rows = [jnp.zeros((1, 128), F32)] * 3
    for part, copy in zip(parts, send_y0):
        copy.wait_recv()
        piece_of = w1[part, :] - not_first * (
            2.0 * p_prev[part, :] + y_prev[part, :] - w0[part, :] + c0 * flow[part, :]
        )
        v[part, :] = piece_of
        factors = (flow[part, :], piece_of, grad[part, :])
        v1_rows = [row + lanes(factor * piece_of) for row, factor in zip(v1_rows, factors)]
    plane[plane_me, pl.ds(5, 3), :] = jnp.concatenate(v1_rows, axis=0)

    def plane_copy(d, shift):
        j, peer = plane_peer(shift)
        send = pltpu.make_async_remote_copy(
            src_ref=plane.at[plane_me], dst_ref=plane.at[plane_me], send_sem=plane_send.at[d],
            recv_sem=plane_recv.at[plane_me], device_id=peer, device_id_type=MESH,
        )
        receive = pltpu.make_async_remote_copy(
            src_ref=plane.at[j], dst_ref=plane.at[j], send_sem=plane_send.at[d],
            recv_sem=plane_recv.at[j], device_id=peer, device_id_type=MESH,
        )
        return send, receive

    plane_copies = [plane_copy(d, shift) for d, shift in enumerate(plane_shifts)]
    for copy, _ in plane_copies:
        copy.start()
    tangent_sweep(from_v, 0, steps - 1)
    for _, copy in plane_copies:
        copy.wait_recv()

    lane = lax.broadcasted_iota(jnp.int32, (16, 128), 1)
    sums = jnp.zeros((16, 128), F32)
    for k in range(planes):
        tile = plane[k * space_count]
        for x in range(1, space_count):
            tile = tile + plane[k * space_count + x]
        sums = jnp.where(lane == k, jnp.sum(tile, axis=1, keepdims=True), sums)
    norm, gf, fv0, vv0, gv0, fv1, vv1, gv1, pp, ss, flux = [sums[r : r + 1] for r in range(11)]
    norm = norm + EPS
    a, b = fv0 / norm, fv1 / norm
    mine = jnp.where(lane[0:1] == lax.div(seg, rows), b, 0.0)
    line[line_me] = jnp.concatenate(
        [pp, vv0 - a * fv0, gv0 - a * gf, ss, vv1 - b * fv1, gv1 - b * gf, flux, mine], axis=0
    )

    def line_copy(d, shift):
        j, peer = line_peer(shift)
        send = pltpu.make_async_remote_copy(
            src_ref=line.at[line_me], dst_ref=line.at[line_me], send_sem=line_send.at[d],
            recv_sem=line_recv.at[line_me], device_id=peer, device_id_type=MESH,
        )
        receive = pltpu.make_async_remote_copy(
            src_ref=line.at[j], dst_ref=line.at[j], send_sem=line_send.at[d],
            recv_sem=line_recv.at[j], device_id=peer, device_id_type=MESH,
        )
        return send, receive

    line_copies = [line_copy(d + 1, shift) for d, shift in enumerate(line_shifts)]
    to_before = pltpu.make_async_remote_copy(
        src_ref=line.at[line_me], dst_ref=line_next, send_sem=line_send.at[0],
        recv_sem=line_next_sem, device_id=(before, space), device_id_type=MESH,
    )
    to_before.start()
    for copy, _ in line_copies:
        copy.start()
    c1 = total(mine)
    from_v[steps] = tangent(steps - 1, from_v[steps - 1] - c1 * from_flow[steps - 1])
    to_before.wait_recv()
    c1_next = total(line_next[7:8])
    for part, copy in zip(parts, send_w1):
        copy.wait_recv()
        s2_out[part, :] = active * (
            2.0 * s1[part, :] + from_v[steps, part, :] - w1_next[part, :] + c1_next * flow_next[part, :]
        )
    for _, copy in line_copies:
        copy.wait_recv()

    whole = line[0]
    for k in range(1, line_size):
        whole = whole + line[k]
    whole = jnp.sum(whole, axis=1, keepdims=True)
    rr, q0, g0, m11, q1, g1, flux = [whole[r : r + 1] for r in range(7)]
    k0 = rr + q0
    k11 = m11 + q1
    alpha0 = rr / k0
    fresh = alpha0 * alpha0 * m11 - rr
    beta = fresh / rr
    more = 1.0 + beta
    alpha1 = fresh / (more * more * k0 - 2.0 * alpha0 * more * m11 + alpha0 * alpha0 * k11)
    sens = flux + alpha0 * g0 + alpha1 * (more * g0 - alpha0 * g1)
    for row, value in enumerate((alpha0 + alpha1 * more, alpha1 * alpha0, sens)):
        coef_out[pl.ds(row, 1), :] = jnp.broadcast_to(value, (1, 128))

    for copies in (send_flow, send_p0, send_w0, send_y0, send_w1):
        for copy in copies:
            copy.wait_send()
    for copy, _ in near_copies + plane_copies + line_copies:
        copy.wait_send()
    to_before.wait_send()


def combine(p0, s1, s2, coef, mult_out, res_out, sens_out):
    along, across = coef[0:1, 0:1], coef[1:2, 0:1]
    sens_out[...] = coef[2:3, 0:1]
    mult_out[...] = along * p0[...] - across * s1[...]
    res_out[...] = p0[...] - along * s1[...] + across * s2[...]


def on_device(rows, axes, advect, growth, forcing, flux_weight, flow_dir, helmholtz):
    steps, height, width = advect.shape[1], advect.shape[3], advect.shape[4]
    seg_count, space_count = axes
    planes = seg_count // rows
    plane_size = planes * space_count
    field = pltpu.VMEM((height, width), F32)
    steps_bf16 = pltpu.VMEM((steps, height, width), BF16)
    half = width // 2
    dma = pltpu.SemaphoreType.DMA
    shape = (steps, height, width)
    results = pl.pallas_call(
        functools.partial(kernel, (seg_count, space_count, rows)),
        out_shape=(
            pltpu.VMEM((height, width), F32),
            pltpu.VMEM((height, width), F32),
            pltpu.VMEM((height, width), F32),
            pltpu.VMEM((8, 128), F32),
        ),
        in_specs=[pl.BlockSpec(memory_space=pl.ANY)] * 6,
        out_specs=tuple([pl.BlockSpec(memory_space=pltpu.VMEM)] * 4),
        scratch_shapes=[
            steps_bf16, steps_bf16, steps_bf16, steps_bf16,
            pltpu.VMEM((height, height), F32), pltpu.VMEM((4, half, half), BF16),
            pltpu.VMEM((4, height, height), BF16),
            *[pltpu.VMEM((steps + 1, height, width), F32)] * 5, field,
            *[field] * 5,
            pltpu.VMEM((space_count, 8, 128), F32), pltpu.VMEM((space_count, 8, 128), F32),
            pltpu.VMEM((plane_size, 16, 128), F32), pltpu.VMEM((rows, 8, 128), F32), pltpu.VMEM((8, 128), F32), pltpu.VMEM((8, 128), F32),
            dma((3 * steps + 3,)), dma((5, CHUNKS)), dma((5, CHUNKS)),
            dma((2 * space_count - 1,)), dma((space_count,)), dma((space_count,)),
            dma((plane_size,)), dma((plane_size,)), dma((rows,)), dma((rows,)), dma,
        ],
        compiler_params=pltpu.CompilerParams(
            collective_id=0, has_side_effects=True, vmem_limit_bytes=60 << 20
        ),
        cost_estimate=pl.CostEstimate(flops=8_000_000_000, bytes_accessed=6_000_000, transcendentals=0),
    )(
        advect.reshape(shape), growth.reshape(shape), forcing.reshape(shape), flux_weight.reshape(shape),
        flow_dir.reshape(height, width), helmholtz.reshape(height, height),
    )
    mult, res, sens = pl.pallas_call(
        combine,
        out_shape=(
            jax.ShapeDtypeStruct((height, width), F32),
            jax.ShapeDtypeStruct((height, width), F32),
            jax.ShapeDtypeStruct((1, 1), F32),
        ),
        in_specs=[pl.BlockSpec(memory_space=pltpu.VMEM)] * 4,
        out_specs=(pl.BlockSpec(memory_space=pltpu.VMEM),) * 3,
        compiler_params=pltpu.CompilerParams(vmem_limit_bytes=4 << 20),
    )(*results)
    return mult[None, None], res[None, None], sens.reshape(())


def solution(mesh):
    in_specs = (
        P("seg", None, "space", None, None),
        P("seg", None, "space", None, None),
        P("seg", None, "space", None, None),
        P("seg", None, "space", None, None),
        P("seg", "space", None, None),
        P("space", None, None),
    )
    out_specs = (P("seg", "space", None, None), P("seg", "space", None, None), P())
    axes = (mesh.shape["seg"], mesh.shape["space"])
    rows = 16 if axes[0] % 16 == 0 else axes[0]
    return jax.shard_map(
        functools.partial(on_device, rows, axes), mesh=mesh, in_specs=in_specs, out_specs=out_specs, check_vma=False
    )
```

```python
import functools
import math

import jax
import jax.numpy as jnp
from jax import lax
from jax.experimental import pallas as pl
from jax.experimental.pallas import tpu as pltpu
from jax.sharding import PartitionSpec as P

EPS = 1e-06
F32 = jnp.float32
BF16 = jnp.bfloat16
MESH = pl.DeviceIdType.MESH
CHUNKS = 2


def cotangent(angle):
    square = angle * angle
    sine = jnp.ones_like(angle)
    for n in (13, 11, 9, 7, 5, 3):
        sine = 1.0 - square * sine * (1.0 / (n * (n - 1)))
    cosine = jnp.ones_like(angle)
    for n in (14, 12, 10, 8, 6, 4, 2):
        cosine = 1.0 - square * cosine * (1.0 / (n * (n - 1)))
    return cosine / (angle * sine)


def derivative_tables(width):
    half = width // 2
    column = lax.broadcasted_iota(jnp.int32, (8, width), 1)
    apart = jnp.where(column < half, column, width - column)
    inside = jnp.logical_and(apart > 0, apart < half)
    apart = jnp.where(inside, apart, 1)
    step = math.pi / width
    near = cotangent(apart.astype(F32) * step)
    far = cotangent((half - apart).astype(F32) * step)
    sign = jnp.where((column < half) == (apart % 2 == 0), 0.25 / width, -0.25 / width)
    sign = jnp.where(inside, sign, 0.0)
    tables = []
    for row in (sign * (near - far), sign * (near + far)):
        block = jnp.concatenate([row] * (half // 8), axis=0)
        tables.append(pltpu.roll(block, 0, 1, stride=1, stride_axis=0)[:, :half])
    return tables


def dot(a, b):
    return jnp.dot(a, b, preferred_element_type=F32)


def split(x):
    high = x.astype(BF16)
    return high, (x - high.astype(F32)).astype(BF16)


def derive(field, tables):
    half = field.shape[1] // 2
    left, right = field[:, :half], field[:, half:]
    sum_high, sum_low = split(left + right)
    gap_high, gap_low = split(left - right)
    even = dot(sum_high, tables[0]) + dot(sum_low, tables[0]) + dot(sum_high, tables[1])
    odd = dot(gap_high, tables[2]) + dot(gap_low, tables[2]) + dot(gap_high, tables[3])
    return jnp.concatenate([even + odd, even - odd], axis=1)


def mix(matrix, field):
    high, low = split(field)
    return dot(matrix[0], high) + dot(matrix[1], high) + dot(matrix[0], low)


def lanes(product):
    row = jnp.sum(product, axis=0, keepdims=True)
    return sum(row[:, k : k + 128] for k in range(0, row.shape[1], 128))


def total(row):
    return jnp.sum(row, axis=1, keepdims=True)


def kernel(
    groups, advect_in, growth_in, forcing_in, weight_in, flow_in, helm_in,
    p0_out, s1_out, s2_out, coef_out,
    advect, growth, forcing, weight, helm, tables, matrix,
    from_p0, from_s1, from_flow, from_v, from_weight, y0,
    flow_next, p_prev, w0_next, y_prev, w1_next,
    near_own, near_next, early, cross, plane, line, line_next, coef,
    load_sem, send_sem, recv_sem,
    near_send, near_recv, next_recv, cross_send, cross_recv, plane_send, plane_recv, line_send, line_recv, line_next_sem,
):
    seg_count, space_count, rows = groups
    seg, space = lax.axis_index("seg"), lax.axis_index("space")
    after, before = lax.rem(seg + 1, seg_count), lax.rem(seg + seg_count - 1, seg_count)
    steps, height, width = advect.shape
    planes = seg_count // rows
    active = jnp.where(seg < seg_count - 1, 1.0, 0.0).astype(F32)
    not_first = jnp.where(seg > 0, 1.0, 0.0).astype(F32)

    def load(slot, source, target):
        return pltpu.make_async_copy(source, target, load_sem.at[slot])

    def load_forcing(n):
        return load(n, forcing_in.at[n], forcing.at[n])

    def step_loads(n):
        return (
            load(steps + n, advect_in.at[n], advect.at[n]),
            load(2 * steps + n, growth_in.at[n], growth.at[n]),
        )

    p0, w0 = from_p0.at[0], from_p0.at[steps]
    s1, w1 = from_s1.at[0], from_s1.at[steps]
    flow, grad = from_flow.at[0], from_weight.at[steps]
    v = from_v.at[0]

    base = 3 * steps
    load_helm = load(base, helm_in, helm)
    load_flow = load(base + 1, flow_in, flow)
    load_weight = load(base + 2, weight_in, weight)
    load_helm.start()
    load_forcing(0).start()
    for n in range(1, steps):
        for copy in (load_forcing(n), *step_loads(n)):
            copy.start()
    for copy in step_loads(0):
        copy.start()
    load_flow.start()
    load_weight.start()

    plane_me = (seg // rows) * space_count + space
    line_me = lax.rem(seg, rows)
    plane_size, line_size = planes * space_count, rows

    def ring(distance, size):
        return min(distance, size - distance)

    def offsets(first, second):
        pairs = [(a, b) for a in range(first) for b in range(second)][1:]
        return sorted(pairs, key=lambda pair: -ring(pair[0], first) - ring(pair[1], second))

    plane_shifts = offsets(planes, space_count)
    line_shifts = offsets(rows // 2, 2)

    def plane_peer(shift):
        plane_at = lax.rem(lax.div(seg, rows) + shift[0], planes)
        x = lax.rem(space + shift[1], space_count)
        return plane_at * space_count + x, (plane_at * rows + line_me, x)

    def line_peer(shift):
        chip = lax.rem(lax.div(line_me, 2) + shift[0], rows // 2)
        j = chip * 2 + lax.rem(lax.rem(line_me, 2) + shift[1], 2)
        return j, (lax.div(seg, rows) * rows + j, space)

    barrier = pltpu.get_barrier_semaphore()
    greeted = [plane_peer(shift)[1] for shift in plane_shifts]
    greeted += [line_peer(shift)[1] for shift in line_shifts]
    greeted += [(s, lax.rem(space + d, space_count)) for s in (before, after) for d in range(space_count)]
    for peer in greeted:
        pl.semaphore_signal(barrier, inc=1, device_id=peer, device_id_type=MESH)

    piece = height // CHUNKS

    def transfer(kind, source, target, seg_to):
        return [
            pltpu.make_async_remote_copy(
                src_ref=source.at[pl.ds(c * piece, piece), :],
                dst_ref=target.at[pl.ds(c * piece, piece), :],
                send_sem=send_sem.at[kind, c],
                recv_sem=recv_sem.at[kind, c],
                device_id=(seg_to, space),
                device_id_type=MESH,
            )
            for c in range(CHUNKS)
        ]

    parts = [pl.ds(c * piece, piece) for c in range(CHUNKS)]

    def start(copies):
        for copy in copies:
            copy.start()

    def arrived(copies):
        for copy in copies:
            copy.wait_recv()

    send_flow = transfer(0, flow_in, flow_next, before)
    send_p0 = transfer(1, p0, p_prev, after)
    send_w0 = transfer(2, w0, w0_next, before)
    send_y0 = transfer(3, y0, y_prev, after)
    send_w1 = transfer(4, w1, w1_next, before)

    def forward():
        return matrix[0], matrix[1]

    def backward():
        return matrix[2], matrix[3]

    def tangent(n, now, forced=False):
        rate = growth[n].astype(F32)
        speed = advect[n].astype(F32)
        update = now + rate * now - speed * derive(now, [tables[k] for k in range(4)])
        if forced:
            update = update + forcing[n].astype(F32)
        return mix(forward(), update)

    def tangent_pair(n, one, two):
        rate = growth[n].astype(F32)
        speed = advect[n].astype(F32)
        slopes = derive(jnp.concatenate([one, two], axis=0), [tables[k] for k in range(4)])
        updates = [
            now + rate * now - speed * slope
            for now, slope in ((one, slopes[:height]), (two, slopes[height:]))
        ]
        ends = mix(forward(), jnp.concatenate(updates, axis=1))
        return ends[:, :width], ends[:, width:]

    def adjoint_rest(n, pulled):
        rate = growth[n].astype(F32)
        speed = advect[n].astype(F32)
        return pulled + rate * pulled + derive(speed * pulled, [tables[k] for k in range(4)])

    def tangent_sweep(path, first, last):
        @pl.loop(first, last)
        def _(n):
            path[n + 1] = tangent(n, path[n])

    def adjoint_sweep(path):
        @pl.loop(0, steps)
        def _(k):
            path[k + 1] = adjoint_rest(steps - 1 - k, mix(backward(), path[k]))

    def gradient_step(k, flux):
        n = steps - 1 - k
        pulled = mix(backward(), weight[n].astype(F32) + from_weight[k])
        return adjoint_rest(n, pulled), flux + lanes(pulled * forcing[n].astype(F32))

    def put(row, value):
        plane[plane_me, pl.ds(row, 1), :] = value

    for k, table in enumerate(derivative_tables(width)):
        tables[2 * k], tables[2 * k + 1] = split(table)

    load_helm.wait()
    high, low = split(helm[...])
    matrix[0], matrix[1] = high, low
    load_forcing(0).wait()
    from_v[1] = dot(matrix[0], forcing[0]) + dot(matrix[1], forcing[0])
    high, low = split(helm[...].T)
    matrix[2], matrix[3] = high, low
    pl.semaphore_wait(barrier, len(greeted))
    start(send_flow)

    @pl.loop(1, steps)
    def _(n):
        for copy in (load_forcing(n), *step_loads(n)):
            copy.wait()
        from_v[n + 1] = tangent(n, from_v[n], forced=True)

    for part, copy in zip(parts, send_p0):
        p0[part, :] = -active * from_v[steps, part, :]
        copy.start()

    for copy in step_loads(0):
        copy.wait()
    adjoint_sweep(from_p0)
    start(send_w0)
    load_flow.wait()
    load_weight.wait()
    from_weight[0] = jnp.zeros_like(from_weight[0])
    put(0, lanes(flow[...] * flow[...]))

    def near_copy(source, kept, slot, send, receive, to):
        return pltpu.make_async_remote_copy(
            src_ref=source, dst_ref=kept.at[slot], send_sem=send, recv_sem=receive.at[slot],
            device_id=to, device_id_type=MESH,
        )

    def near_group(source, kept, sends, receive, seg_to, first):
        group = []
        for d in range(first, space_count):
            j = lax.rem(space + d, space_count)
            group.append([near_copy(source, kept, s, sends.at[d], receive, (seg_to, j)) for s in (space, j)])
        return group

    own_tile = near_own.at[space]
    own_copies = near_group(own_tile, near_own, near_send.at[0], near_recv, seg, 1)
    v0_copies = near_group(own_tile, near_next, near_send.at[1], next_recv, before, 0)
    w0_copies = near_group(early, near_next, near_send.at[1], next_recv, before, 0)
    cross_copies = near_group(cross.at[space], cross, cross_send, cross_recv, seg, 1)

    def near_ratio(row, kept, less=None):
        sums = kept[0]
        for x in range(1, space_count):
            sums = sums + kept[x]
        top = total(sums[1:2])
        if less is not None:
            rows_less = less[0]
            for x in range(1, space_count):
                rows_less = rows_less + less[x]
            top = top - total(rows_less[1:2])
        c = top / (total(sums[0:1]) + EPS)
        coef[pl.ds(row, 1), :] = jnp.broadcast_to(c, (1, 128))

    def flow_tile(row):
        return jnp.concatenate([plane[plane_me, pl.ds(0, 1), :], row, jnp.zeros((6, 128), F32)], axis=0)

    def begin_v0():
        row = jnp.zeros((1, 128), F32)
        for part, copy in zip(parts, send_p0):
            copy.wait_recv()
            piece_of = w0[part, :] - p_prev[part, :]
            v[part, :] = piece_of
            row = row + lanes(flow[part, :] * piece_of)
        put(2, row)
        near_own[space] = flow_tile(row)
        for copy, _ in own_copies:
            copy.start()

    def v0_sums():
        put(1, lanes(grad[...] * flow[...]))
        put(3, lanes(v[...] * v[...]))
        put(4, lanes(grad[...] * v[...]))
        put(8, lanes(p0[...] * p0[...]))
        plane[plane_me, pl.ds(11, 5), :] = jnp.zeros((5, 128), F32)

    def own_ratio():
        for _, copy in own_copies:
            copy.wait_recv()
        near_ratio(0, near_own)
        return coef[0:1, 0:1]

    second = lax.rem(seg, 2) == 1

    @pl.when(second)
    def _():
        begin_v0()
        for copy, _ in v0_copies:
            copy.start()

        @pl.loop(0, steps - 1)
        def _(n):
            one, two = tangent_pair(n, from_v[n], from_flow[n])
            from_v[n + 1] = one
            from_flow[n + 1] = two

        y0[...] = tangent(steps - 1, from_v[steps - 1] - own_ratio() * from_flow[steps - 1])
        start(send_y0)
        arrived(send_flow)
        cross[space] = flow_tile(lanes(flow_next[...] * p0[...]))
        for copy, _ in cross_copies:
            copy.start()

        def body(k, flux):
            now, flux = gradient_step(k, flux)
            from_weight[k + 1] = now
            return flux

        put(10, lax.fori_loop(0, steps, body, jnp.zeros((1, 128), F32)))
        v0_sums()
        for _, copy in v0_copies + cross_copies:
            copy.wait_recv()
        near_ratio(1, near_next, less=cross)

    @pl.when(jnp.logical_not(second))
    def _():
        early[...] = flow_tile(lanes(flow[...] * w0[...]))
        for copy, _ in w0_copies:
            copy.start()

        def body(k, flux):
            one = tangent(k, from_flow[k])
            now, flux = gradient_step(k, flux)
            from_flow[k + 1] = one
            from_weight[k + 1] = now
            return flux

        put(10, lax.fori_loop(0, steps, body, jnp.zeros((1, 128), F32)))
        begin_v0()
        tangent_sweep(from_v, 0, steps)
        v0_sums()
        c0 = own_ratio()
        for part, copy in zip(parts, send_y0):
            y0[part, :] = from_v[steps, part, :] - c0 * from_flow[steps, part, :]
            copy.start()
        for _, copy in v0_copies:
            copy.wait_recv()
        near_ratio(1, near_next)
        arrived(send_flow)

    c0, c0_next = coef[0:1, 0:1], coef[1:2, 0:1]
    row = jnp.zeros((1, 128), F32)
    for part, copy in zip(parts, send_w0):
        copy.wait_recv()
        piece_of = active * (
            2.0 * p0[part, :] + y0[part, :] - w0_next[part, :] + c0_next * flow_next[part, :]
        )
        s1[part, :] = piece_of
        row = row + lanes(piece_of * piece_of)
    put(9, row)
    adjoint_sweep(from_s1)
    start(send_w1)
    p0_out[...] = p0[...]
    s1_out[...] = s1[...]

    v1_rows = [jnp.zeros((1, 128), F32)] * 3
    for part, copy in zip(parts, send_y0):
        copy.wait_recv()
        piece_of = w1[part, :] - not_first * (
            2.0 * p_prev[part, :] + y_prev[part, :] - w0[part, :] + c0 * flow[part, :]
        )
        v[part, :] = piece_of
        factors = (flow[part, :], piece_of, grad[part, :])
        v1_rows = [row + lanes(factor * piece_of) for row, factor in zip(v1_rows, factors)]
    plane[plane_me, pl.ds(5, 3), :] = jnp.concatenate(v1_rows, axis=0)

    def plane_copy(d, shift):
        j, peer = plane_peer(shift)
        send = pltpu.make_async_remote_copy(
            src_ref=plane.at[plane_me], dst_ref=plane.at[plane_me], send_sem=plane_send.at[d],
            recv_sem=plane_recv.at[plane_me], device_id=peer, device_id_type=MESH,
        )
        receive = pltpu.make_async_remote_copy(
            src_ref=plane.at[j], dst_ref=plane.at[j], send_sem=plane_send.at[d],
            recv_sem=plane_recv.at[j], device_id=peer, device_id_type=MESH,
        )
        return send, receive

    plane_copies = [plane_copy(d, shift) for d, shift in enumerate(plane_shifts)]
    for copy, _ in plane_copies:
        copy.start()
    tangent_sweep(from_v, 0, steps - 1)
    for _, copy in plane_copies:
        copy.wait_recv()

    lane = lax.broadcasted_iota(jnp.int32, (16, 128), 1)
    sums = jnp.zeros((16, 128), F32)
    for k in range(planes):
        tile = plane[k * space_count]
        for x in range(1, space_count):
            tile = tile + plane[k * space_count + x]
        sums = jnp.where(lane == k, jnp.sum(tile, axis=1, keepdims=True), sums)
    norm, gf, fv0, vv0, gv0, fv1, vv1, gv1, pp, ss, flux = [sums[r : r + 1] for r in range(11)]
    norm = norm + EPS
    a, b = fv0 / norm, fv1 / norm
    mine = jnp.where(lane[0:1] == lax.div(seg, rows), b, 0.0)
    line[line_me] = jnp.concatenate(
        [pp, vv0 - a * fv0, gv0 - a * gf, ss, vv1 - b * fv1, gv1 - b * gf, flux, mine], axis=0
    )

    def line_copy(d, shift):
        j, peer = line_peer(shift)
        send = pltpu.make_async_remote_copy(
            src_ref=line.at[line_me], dst_ref=line.at[line_me], send_sem=line_send.at[d],
            recv_sem=line_recv.at[line_me], device_id=peer, device_id_type=MESH,
        )
        receive = pltpu.make_async_remote_copy(
            src_ref=line.at[j], dst_ref=line.at[j], send_sem=line_send.at[d],
            recv_sem=line_recv.at[j], device_id=peer, device_id_type=MESH,
        )
        return send, receive

    line_copies = [line_copy(d + 1, shift) for d, shift in enumerate(line_shifts)]
    to_before = pltpu.make_async_remote_copy(
        src_ref=line.at[line_me], dst_ref=line_next, send_sem=line_send.at[0],
        recv_sem=line_next_sem, device_id=(before, space), device_id_type=MESH,
    )
    to_before.start()
    for copy, _ in line_copies:
        copy.start()
    c1 = total(mine)
    from_v[steps] = tangent(steps - 1, from_v[steps - 1] - c1 * from_flow[steps - 1])
    to_before.wait_recv()
    c1_next = total(line_next[7:8])
    for part, copy in zip(parts, send_w1):
        copy.wait_recv()
        s2_out[part, :] = active * (
            2.0 * s1[part, :] + from_v[steps, part, :] - w1_next[part, :] + c1_next * flow_next[part, :]
        )
    for _, copy in line_copies:
        copy.wait_recv()

    whole = line[0]
    for k in range(1, line_size):
        whole = whole + line[k]
    whole = jnp.sum(whole, axis=1, keepdims=True)
    rr, q0, g0, m11, q1, g1, flux = [whole[r : r + 1] for r in range(7)]
    k0 = rr + q0
    k11 = m11 + q1
    alpha0 = rr / k0
    fresh = alpha0 * alpha0 * m11 - rr
    beta = fresh / rr
    more = 1.0 + beta
    alpha1 = fresh / (more * more * k0 - 2.0 * alpha0 * more * m11 + alpha0 * alpha0 * k11)
    sens = flux + alpha0 * g0 + alpha1 * (more * g0 - alpha0 * g1)
    for row, value in enumerate((alpha0 + alpha1 * more, alpha1 * alpha0, sens)):
        coef_out[pl.ds(row, 1), :] = jnp.broadcast_to(value, (1, 128))

    for copies in (send_flow, send_p0, send_w0, send_y0, send_w1):
        for copy in copies:
            copy.wait_send()
    for copy, _ in own_copies + v0_copies + plane_copies + line_copies:
        copy.wait_send()

    @pl.when(second)
    def _():
        for copy, _ in cross_copies:
            copy.wait_send()

    to_before.wait_send()


def combine(p0, s1, s2, coef, mult_out, res_out, sens_out):
    along, across = coef[0:1, 0:1], coef[1:2, 0:1]
    sens_out[...] = coef[2:3, 0:1]
    mult_out[...] = along * p0[...] - across * s1[...]
    res_out[...] = p0[...] - along * s1[...] + across * s2[...]


def on_device(rows, axes, advect, growth, forcing, flux_weight, flow_dir, helmholtz):
    steps, height, width = advect.shape[1], advect.shape[3], advect.shape[4]
    seg_count, space_count = axes
    planes = seg_count // rows
    plane_size = planes * space_count
    field = pltpu.VMEM((height, width), F32)
    steps_bf16 = pltpu.VMEM((steps, height, width), BF16)
    half = width // 2
    dma = pltpu.SemaphoreType.DMA
    shape = (steps, height, width)
    results = pl.pallas_call(
        functools.partial(kernel, (seg_count, space_count, rows)),
        out_shape=(
            pltpu.VMEM((height, width), F32),
            pltpu.VMEM((height, width), F32),
            pltpu.VMEM((height, width), F32),
            pltpu.VMEM((8, 128), F32),
        ),
        in_specs=[pl.BlockSpec(memory_space=pl.ANY)] * 6,
        out_specs=tuple([pl.BlockSpec(memory_space=pltpu.VMEM)] * 4),
        scratch_shapes=[
            steps_bf16, steps_bf16, steps_bf16, steps_bf16,
            pltpu.VMEM((height, height), F32), pltpu.VMEM((4, half, half), BF16),
            pltpu.VMEM((4, height, height), BF16),
            *[pltpu.VMEM((steps + 1, height, width), F32)] * 5, field,
            *[field] * 5,
            pltpu.VMEM((space_count, 8, 128), F32), pltpu.VMEM((space_count, 8, 128), F32),
            pltpu.VMEM((8, 128), F32), pltpu.VMEM((space_count, 8, 128), F32),
            pltpu.VMEM((plane_size, 16, 128), F32), pltpu.VMEM((rows, 8, 128), F32), pltpu.VMEM((8, 128), F32), pltpu.VMEM((8, 128), F32),
            dma((3 * steps + 3,)), dma((5, CHUNKS)), dma((5, CHUNKS)),
            dma((2, space_count)), dma((space_count,)), dma((space_count,)), dma((space_count,)), dma((space_count,)),
            dma((plane_size,)), dma((plane_size,)), dma((rows,)), dma((rows,)), dma,
        ],
        compiler_params=pltpu.CompilerParams(
            collective_id=0, has_side_effects=True, vmem_limit_bytes=60 << 20
        ),
        cost_estimate=pl.CostEstimate(flops=8_000_000_000, bytes_accessed=6_000_000, transcendentals=0),
    )(
        advect.reshape(shape), growth.reshape(shape), forcing.reshape(shape), flux_weight.reshape(shape),
        flow_dir.reshape(height, width), helmholtz.reshape(height, height),
    )
    mult, res, sens = pl.pallas_call(
        combine,
        out_shape=(
            jax.ShapeDtypeStruct((height, width), F32),
            jax.ShapeDtypeStruct((height, width), F32),
            jax.ShapeDtypeStruct((1, 1), F32),
        ),
        in_specs=[pl.BlockSpec(memory_space=pltpu.VMEM)] * 4,
        out_specs=(pl.BlockSpec(memory_space=pltpu.VMEM),) * 3,
        compiler_params=pltpu.CompilerParams(vmem_limit_bytes=4 << 20),
    )(*results)
    return mult[None, None], res[None, None], sens.reshape(())


def solution(mesh):
    in_specs = (
        P("seg", None, "space", None, None),
        P("seg", None, "space", None, None),
        P("seg", None, "space", None, None),
        P("seg", None, "space", None, None),
        P("seg", "space", None, None),
        P("space", None, None),
    )
    out_specs = (P("seg", "space", None, None), P("seg", "space", None, None), P())
    axes = (mesh.shape["seg"], mesh.shape["space"])
    rows = 16 if axes[0] % 16 == 0 else axes[0]
    return jax.shard_map(
        functools.partial(on_device, rows, axes), mesh=mesh, in_specs=in_specs, out_specs=out_specs, check_vma=False
    )
```
